32 devices in a mesh: sx: 4 (over y, x), sy: 8 (over z, core).
Axes of the slice: x: 2, y: 2, z: 4, core: 2. Of those that a mesh axis runs over, the one named last changes fastest.
Arguments:
- scalar_field: float32 [128, 256, 512], P('sx', 'sy'), may hold values from -4 to 7
- diffusivity: float32 [128, 256, 512], P('sx', 'sy'), may hold values from 0.03 to 0.11
- reaction_rate: float32 [128, 256, 512], P('sx', 'sy'), may hold values from 0.05 to 0.5
- shear_offsets: int32 [4, 256], replicated, may hold values from 0 to 31
- depth_order: int32 [4, 512], replicated, may hold values from 0 to 1
- tf_centres: float32 [8], replicated, may hold values from -2 to 2
- tf_colour: float32 [3, 8], replicated, may hold values from 0.5 to 2
- tf_opacity: float32 [8], replicated, may hold values from 0.001953125 to 0.01953125
Outputs:
- field_out: float32 [128, 256, 512], P('sx', 'sy')
- image: float32 [4, 3, 128, 512], P(None, None, ('sx', 'sy'))
- transmittance: float32 [4, 128, 512], P(None, ('sx', 'sy'))
The draws below stay inside these ranges and needn't reach their ends.
All inputs are finite; a program needn't handle non-finite values.
Results may differ from the reference program's by a relative error of at most 0.0002.
Values sent between devices are 32-bit elements; how exact they have to be, the bound alone decides.
A program may use at most 128 MiB of HBM per device.

```python
import math
import jax
import jax.numpy as jnp
from jax import lax

CX = 32
NZ = 512
STEPS = 4
VIEWS = 4
BUMPS = 8
MAXSHIFT = 8
NX = 128
NY = 256


def draw_scalar_field(key, part):
    plane_key = jax.random.fold_in(key, 11)
    cell_key = jax.random.fold_in(key, 23)
    plane_shift = jax.random.uniform(plane_key, (NY,), jnp.float32, -1.5, 1.5)
    jitter_values = 0.8 * jax.random.normal(cell_key, (NX, NY, NZ), jnp.float32)
    return jnp.clip(plane_shift[None, :, None] + jitter_values, -4.0, 7.0)


def plant(entries, own_key, low, largest):
    dims = entries.shape
    index_at = [jax.random.randint(jax.random.fold_in(own_key, axis), (), 0, dims[axis]) for axis in range(len(dims))]
    entries = entries.at[tuple(index_at)].set(low)
    longest = dims.index(max(dims))
    index_at[longest] = (index_at[longest] + 1) % dims[longest]
    return entries.at[tuple(index_at)].set(largest)


def shard_levels(rng, dims, cuts, least, top_value):
    def one(axis_at, blocks):
        draws = jax.random.uniform(jax.random.fold_in(jax.random.fold_in(rng, 6), axis_at), (blocks,), jnp.float32, least / len(cuts), top_value / len(cuts))
        return jnp.repeat(jnp.exp(draws), dims[axis_at] // blocks).reshape((-1,) + (1,) * (len(dims) - axis_at - 1))

    loudness = one(*cuts[0])
    for cut in cuts[1:]:
        loudness = loudness * one(*cut)
    return loudness


def setup_inputs(seed: int = 0) -> dict:
    key_list = jax.random.split(jax.random.key(seed), 9)
    scalar_field = draw_scalar_field(jax.random.fold_in(key_list[8], 71), 0)
    diffusivity = jnp.clip(jnp.exp(math.log(0.11) - 1.299283 * jax.random.uniform(key_list[1], (NX, NY, NZ), jnp.float32) ** shard_levels(key_list[1], (NX, NY, NZ), ((0, 4), (1, 8)), -0.2, 0.2)), 0.03, 0.11)
    reaction_rate = jnp.clip(jnp.exp(math.log(0.5) - 2.3025851 * jax.random.uniform(key_list[2], (NX, NY, NZ), jnp.float32) ** shard_levels(key_list[2], (NX, NY, NZ), ((0, 4), (1, 8)), -0.2, 0.2)), 0.05, 0.5)
    shear_offsets = plant(jax.random.randint(key_list[3], (VIEWS, NY), 0, 4 * MAXSHIFT), jax.random.fold_in(key_list[3], 1), 0, (4 * MAXSHIFT) - 1).astype(jnp.int32)
    depth_order = plant(jax.random.randint(key_list[4], (VIEWS, NZ), 0, 2), jax.random.fold_in(key_list[4], 1), 0, 1).astype(jnp.int32)
    tf_centres = jnp.clip(jax.random.uniform(key_list[5], (BUMPS,), jnp.float32, -2.0, 2.0), -2.0, 2.0)
    tf_colour = jnp.clip(jnp.exp(jax.random.uniform(key_list[6], (3, BUMPS), jnp.float32, math.log(0.5), math.log(2.0))), 0.5, 2.0)
    tf_opacity = jnp.clip(jnp.exp(jax.random.uniform(key_list[7], (BUMPS,), jnp.float32, math.log(0.001953125), math.log(0.01953125))), 0.001953125, 0.01953125)
    return dict(scalar_field=scalar_field, diffusivity=diffusivity, reaction_rate=reaction_rate, shear_offsets=shear_offsets, depth_order=depth_order, tf_centres=tf_centres, tf_colour=tf_colour, tf_opacity=tf_opacity)


diff_gain = 0.4
bump_sharpness = 2.0


def neighbour_flux(field_pad, diff_pad):
    centre_cut = (slice(1, -1), slice(1, -1), slice(1, -1))
    neighbours = [
        (slice(2, None), slice(1, -1), slice(1, -1)),
        (slice(None, -2), slice(1, -1), slice(1, -1)),
        (slice(1, -1), slice(2, None), slice(1, -1)),
        (slice(1, -1), slice(None, -2), slice(1, -1)),
        (slice(1, -1), slice(1, -1), slice(2, None)),
        (slice(1, -1), slice(1, -1), slice(None, -2)),
    ]
    centre_field = field_pad[centre_cut]
    centre_diff = diff_pad[centre_cut]
    change = jnp.zeros_like(centre_field)
    for cut in neighbours:
        change = change + 0.5 * (centre_diff + diff_pad[cut]) * (field_pad[cut] - centre_field)
    return change


def shear_view(field_block, offsets):
    z_cells = field_block.shape[2]
    whole_cells = (offsets // 4).astype(jnp.int32)
    fraction = (offsets % 4).astype(jnp.float32) * 0.25
    padded = jnp.pad(field_block, ((0, 0), (0, 0), (0, MAXSHIFT + 1)))
    window = jax.vmap(lambda plane, start: lax.dynamic_slice_in_dim(plane, start, z_cells + 1, 1), in_axes=(1, 0), out_axes=1)(padded, whole_cells)
    fraction = fraction[None, :, None]
    return (1.0 - fraction) * window[:, :, :z_cells] + fraction * window[:, :, 1:]


def transfer(sheared, tf_centres, tf_colour, tf_opacity):
    optical = jnp.zeros_like(sheared)
    colours = [jnp.zeros_like(sheared) for channel in range(3)]
    for bump_index in range(tf_centres.shape[0]):
        bump_value = jnp.exp(-jnp.square(bump_sharpness * (sheared - tf_centres[bump_index])))
        optical = optical + tf_opacity[bump_index] * bump_value
        colours = [colours[channel] + tf_colour[channel, bump_index] * bump_value for channel in range(3)]
    return optical, colours


def render_block(field_block, shear_offsets, depth_order, tf_centres, tf_colour, tf_opacity):
    images = []
    lights = []
    for viewer in range(VIEWS):
        sheared = shear_view(field_block, shear_offsets[viewer])
        optical, colours = transfer(sheared, tf_centres, tf_colour, tf_opacity)
        running = jnp.cumsum(optical, axis=1)
        total = running[:, -1:, :]
        rising = (depth_order[viewer] == 0)[None, None, :]
        before = jnp.where(rising, running - optical, total - running)
        weight = (1.0 - jnp.exp(-optical)) * jnp.exp(-before)
        images.append(jnp.stack([jnp.sum(channel * weight, axis=1) for channel in colours]))
        lights.append(jnp.exp(-total[:, 0, :]))
    return jnp.stack(images), jnp.stack(lights)


def reference(scalar_field, diffusivity, reaction_rate, shear_offsets, depth_order, tf_centres, tf_colour, tf_opacity):
    field_now = scalar_field
    for iteration in range(STEPS):
        diff_now = diffusivity * (1.0 + diff_gain * jnp.tanh(field_now))
        change = neighbour_flux(jnp.pad(field_now, 1), jnp.pad(diff_now, 1))
        field_now = field_now + change + reaction_rate * jnp.tanh(field_now)
    blocks = field_now.reshape(NX // CX, CX, NY, NZ)
    images, lights = lax.map(lambda block: render_block(block, shear_offsets, depth_order, tf_centres, tf_colour, tf_opacity), blocks)
    image = jnp.transpose(images, (1, 2, 0, 3, 4)).reshape(VIEWS, 3, NX, NZ)
    transmittance = jnp.transpose(lights, (1, 0, 2, 3)).reshape(VIEWS, NX, NZ)
    return field_now, image, transmittance
```

```python
import functools
import math

import jax
import jax.numpy as jnp
from jax import lax
from jax.experimental import pallas as pl
from jax.experimental.pallas import tpu as pltpu
from jax.sharding import PartitionSpec as P

STEPS = 4
DIFF_GAIN = 0.4
SHARPNESS = 2.0
LOG2E = math.log2(math.e)
SCALE = SHARPNESS * math.sqrt(LOG2E)
MESH = pl.DeviceIdType.MESH
LANES = 128
SUB = 8
UNROLL = 2
WIDE = 2


def conduct(diff, field):
    return diff * (1.0 + DIFF_GAIN * jnp.tanh(field))


def kernel(
    n_x, n_y,
    u_ref, d_ref, r_ref, off_ref, ord_ref, cen_ref, col_ref, opa_ref,
    f_ref, img_ref, tr_ref,
    field, cond, x_lo, x_hi, dx_lo, dx_hi, p_lo, p_hi, y_lo, y_hi,
    dp_lo, dp_hi, dy_lo, dy_hi, del_lo, del_hi, tall, slope,
    part, got, sgn_ref, c2_ref, wop_ref, wcol_ref,
    halo_send, halo_recv, part_send, part_recv, out_sem,
):
    nx, ny, nz = u_ref.shape
    views = ord_ref.shape[0]
    bumps = cen_ref.shape[0]
    ztiles = nz // LANES
    rows = part.shape[4]
    per_group = SUB // rows
    groups = nx // SUB
    ix, iy = lax.axis_index("sx"), lax.axis_index("sy")

    barrier = pltpu.get_barrier_semaphore()
    for hop in range(1, n_y):
        pl.semaphore_signal(
            barrier, inc=1, device_id={"sy": lax.rem(iy + hop, n_y)}, device_id_type=MESH)

    @pl.when(ix > 0)
    def _():
        pl.semaphore_signal(barrier, inc=1, device_id={"sx": ix - 1}, device_id_type=MESH)

    @pl.when(ix < n_x - 1)
    def _():
        pl.semaphore_signal(barrier, inc=1, device_id={"sx": ix + 1}, device_id_type=MESH)

    sides = [
        (ix > 0, {"sx": ix - 1}, 0, 1),
        (ix < n_x - 1, {"sx": ix + 1}, 1, 0),
        (iy > 0, {"sy": iy - 1}, 2, 3),
        (iy < n_y - 1, {"sy": iy + 1}, 3, 2),
    ]
    landings = [x_lo, x_hi, y_lo, y_hi]
    diff_landings = [dx_lo, dx_hi, dy_lo, dy_hi]

    def halo(step, side):
        exists, neighbour, here, there = sides[side]
        if step == STEPS:
            src = [d_ref.at[0], d_ref.at[nx - 1], dp_lo, dp_hi][side]
            dst, own = diff_landings[there], diff_landings[here]
        else:
            now = step % 2
            src = [
                field.at[now, 0, pl.ds(0, ny)], field.at[now, nx - 1, pl.ds(0, ny)],
                p_lo.at[step], p_hi.at[step],
            ][side]
            dst, own = landings[there].at[step], landings[here].at[step]
        go = pltpu.make_async_remote_copy(
            src_ref=src, dst_ref=dst, send_sem=halo_send.at[step, here],
            recv_sem=halo_recv.at[step, there], device_id=neighbour, device_id_type=MESH)
        come = pltpu.make_async_remote_copy(
            src_ref=src, dst_ref=own, send_sem=halo_send.at[step, here],
            recv_sem=halo_recv.at[step, here], device_id=neighbour, device_id_type=MESH)
        return exists, go, come

    def start_halos(step):
        for side in range(4):
            exists, go, _ = halo(step, side)
            pl.when(exists)(go.start)

    def wait_halos(step):
        for side in range(4):
            exists, go, come = halo(step, side)

            @pl.when(exists)
            def _():
                come.wait_recv()
                go.wait_send()

    for side in range(4):
        @pl.when(jnp.logical_not(sides[side][0]))
        def _():
            landings[side][...] = jnp.zeros_like(landings[side])
            diff_landings[side][...] = jnp.zeros_like(diff_landings[side])

    @pl.loop(0, groups)
    def _(block):
        base = pl.multiple_of(block * SUB, SUB)
        for ref, row, out in (
            (u_ref, 0, p_lo.at[0]), (u_ref, ny - 1, p_hi.at[0]),
            (d_ref, 0, dp_lo), (d_ref, ny - 1, dp_hi),
        ):
            out[pl.ds(base, SUB), :] = jnp.concatenate(
                [ref[base + j, row:row + 1, :] for j in range(SUB)], axis=0)

    @pl.loop(0, nx)
    def _(x):
        for t in range(ny // SUB):
            cut = pl.ds(t * SUB, SUB)
            now = u_ref[x, cut, :]
            field[0, x, cut, :] = now
            cond[x, cut, :] = conduct(d_ref[x, cut, :], now)

    arrivals = (n_y - 1) + (ix > 0).astype(jnp.int32) + (ix < n_x - 1).astype(jnp.int32)
    pl.semaphore_wait(barrier, arrivals)
    start_halos(0)
    start_halos(STEPS)

    row_at = lax.broadcasted_iota(jnp.int32, (SUB, nz), 0)
    col_at = lax.broadcasted_iota(jnp.int32, (SUB, nz), 1)

    for step in range(STEPS):
        now, later = step % 2, (step + 1) % 2
        if step:
            @pl.loop(0, nx)
            def _(x):
                for t in range(ny // SUB):
                    cut = pl.ds(t * SUB, SUB)
                    cond[x, cut, :] = conduct(d_ref[x, cut, :], field[now, x, cut, :])

        @pl.loop(0, nx)
        def _(x):
            below, above = jnp.maximum(x - 1, 0), jnp.minimum(x + 1, nx - 1)
            carried = None
            for t in range(ny // SUB):
                cut, shifted = pl.ds(t * SUB, SUB), pl.ds(t * SUB + 1, SUB)
                u, k = field[now, x, cut, :], cond[x, cut, :]
                change = (k + cond[below, cut, :]) * (field[now, below, cut, :] - u)
                change += (k + cond[above, cut, :]) * (field[now, above, cut, :] - u)
                flux = (k + cond[x, shifted, :]) * (field[now, x, shifted, :] - u)
                if t == ny // SUB - 1:
                    flux = jnp.where(row_at == SUB - 1, 0.0, flux)
                turned = pltpu.roll(flux, 1, 0)
                change += flux - jnp.where(row_at == 0, 0.0 if t == 0 else carried, turned)
                carried = turned
                ku = k * u
                right_u, right_k = pltpu.roll(u, nz - 1, 1), pltpu.roll(k, nz - 1, 1)
                flux = jnp.where(col_at == nz - 1, -ku, (k + right_k) * (right_u - u))
                change += flux - jnp.where(col_at == 0, ku, pltpu.roll(flux, 1, 1))
                field[later, x, cut, :] = u + 0.5 * change + r_ref[x, cut, :] * jnp.tanh(u)

        if step == 0:
            wait_halos(STEPS)
        wait_halos(step)
        inner = pl.ds(0, ny)
        for x, land, diff in ((0, x_lo, dx_lo), (nx - 1, x_hi, dx_hi)):
            beside = land[step]
            field[later, x, inner, :] += (
                0.5 * (cond[x, inner, :] + conduct(diff[...], beside))
                * (beside - field[now, x, inner, :]))
        for packed, own, land, diff, out in (
            (p_lo, dp_lo, y_lo, dy_lo, del_lo), (p_hi, dp_hi, y_hi, dy_hi, del_hi),
        ):
            u, beside = packed[step], land[step]
            out[...] = 0.5 * (conduct(own[...], u) + conduct(diff[...], beside)) * (beside - u)

        @pl.loop(0, groups)
        def _(block):
            base = pl.multiple_of(block * SUB, SUB)
            for packed, delta, row in ((p_lo, del_lo, 0), (p_hi, del_hi, ny - 1)):
                extra = delta[pl.ds(base, SUB), :]
                edge = []
                for j in range(SUB):
                    value = field[later, base + j, row:row + 1, :] + extra[j:j + 1, :]
                    field[later, base + j, row:row + 1, :] = value
                    edge.append(value)
                if step < STEPS - 1:
                    packed[step + 1, pl.ds(base, SUB), :] = jnp.concatenate(edge, axis=0)

        if step < STEPS - 1:
            start_halos(step + 1)

    last = STEPS % 2
    out_copy = pltpu.make_async_copy(field.at[last, :, pl.ds(0, ny)], f_ref, out_sem)
    out_copy.start()

    for ref in (tall, slope):
        ref[ztiles] = jnp.zeros_like(ref[ztiles])

    @pl.loop(0, nx)
    def _(x):
        for t in range(ny // SUB):
            value = field[last, x, pl.ds(t * SUB, SUB), :] * SCALE
            rise = jnp.where(col_at == nz - 1, 0.0, pltpu.roll(value, nz - 1, 1)) - value
            for tile in range(ztiles):
                lanes = slice(tile * LANES, (tile + 1) * LANES)
                spot = pl.ds(t * SUB * nx + x, SUB, stride=nx)
                tall[tile, spot, :] = value[:, lanes]
                slope[tile, spot, :] = rise[:, lanes]

    for view in range(views):
        for tile in range(ztiles):
            order = ord_ref[view:view + 1, tile * LANES:(tile + 1) * LANES]
            sign = jnp.where(order == 0, -1.0, 1.0)
            sgn_ref[view * ztiles + tile] = jnp.broadcast_to(sign, (SUB, LANES))
    for bump in range(bumps):
        centre = jnp.full((SUB, LANES), cen_ref[bump] * SCALE, jnp.float32)
        factor = jnp.exp2(-centre * centre)
        c2_ref[bump] = 2.0 * centre
        wop_ref[bump] = opa_ref[bump] * factor
        for channel in range(3):
            wcol_ref[channel, bump] = col_ref[channel, bump] * factor

    lane = lax.broadcasted_iota(jnp.int32, (SUB, LANES), 1)
    pairs = ztiles // WIDE

    def render(group, view, first):
        rate = [sgn_ref[view * ztiles + first + a] * LOG2E for a in range(WIDE)]

        def plane(y, carry):
            offset = off_ref[view, iy * ny + y]
            whole = offset >> 2
            frac = (offset & 3).astype(jnp.float32) * 0.25
            spot = pl.ds(pl.multiple_of(y * nx + group * SUB, SUB), SUB)
            turned = []
            for a in range(WIDE + 1):
                mixed = tall[first + a, spot, :] + frac * slope[first + a, spot, :]
                turned.append(pltpu.roll(mixed, (LANES - whole) & (LANES - 1), 1))
            inside = lane < LANES - whole
            result = []
            for a in range(WIDE):
                sums, depth, light = carry[a]
                s = jnp.where(inside, turned[a], turned[a + 1])
                bump = [jnp.exp2(s * (c2_ref[b] - s)) for b in range(bumps)]
                terms = [wop_ref[b] * bump[b] for b in range(bumps)]
                while len(terms) > 1:
                    terms = [i + j for i, j in zip(terms[::2], terms[1::2])]
                depth = depth + terms[0]
                new = jnp.exp2(rate[a] * depth)
                step = new - light
                sums = tuple(sums[b] + step * bump[b] for b in range(bumps))
                result.append((sums, depth, new))
            return tuple(result)

        def several(i, carry):
            for j in range(UNROLL):
                carry = plane(i * UNROLL + j, carry)
            return carry

        zero = jnp.zeros((SUB, LANES), jnp.float32)
        start = tuple(((zero,) * bumps, zero, zero + 1.0) for a in range(WIDE))
        ended = lax.fori_loop(0, ny // UNROLL, several, start)
        for a in range(WIDE):
            sums, depth, light = ended[a]
            sign = sgn_ref[view * ztiles + first + a]
            factor = jnp.where(sign > 0.0, jnp.exp(-depth), -1.0)
            values = []
            for channel in range(3):
                total = wcol_ref[channel, 0] * sums[0]
                for b in range(1, bumps):
                    total += wcol_ref[channel, b] * sums[b]
                values.append(total * factor)
            values.append(depth)
            for j in range(per_group):
                for channel, value in enumerate(values):
                    part[group * per_group + j, view, channel, first + a] = (
                        value[j * rows:(j + 1) * rows])

    def share(owner):
        return pltpu.make_async_remote_copy(
            src_ref=part.at[owner], dst_ref=got.at[iy], send_sem=part_send.at[owner],
            recv_sem=part_recv.at[iy], device_id={"sy": owner}, device_id_type=MESH)

    own_group = iy // per_group

    @pl.loop(0, groups)
    def _(turn):
        group = lax.rem(own_group + 1 + turn, groups)

        @pl.loop(0, views * pairs)
        def _(item):
            render(group, item // pairs, lax.rem(item, pairs) * WIDE)

        for j in range(per_group):
            owner = group * per_group + j

            @pl.when(owner != iy)
            def _():
                share(owner).start()

            @pl.when(owner == iy)
            def _():
                got[iy] = part[iy]

    for other in range(n_y):
        @pl.when(other != iy)
        def _():
            pltpu.make_async_remote_copy(
                src_ref=part.at[other], dst_ref=got.at[other], send_sem=part_send.at[other],
                recv_sem=part_recv.at[other], device_id={"sy": other}, device_id_type=MESH,
            ).wait_recv()

    for view in range(views):
        for tile in range(ztiles):
            lanes = slice(tile * LANES, (tile + 1) * LANES)
            rising = sgn_ref[view * ztiles + tile][:rows] < 0.0
            depths = [got[source, view, 3, tile] for source in range(n_y)]
            total = depths[0]
            for depth in depths[1:]:
                total = total + depth
            front = jnp.zeros_like(total)
            image = [jnp.zeros_like(total)] * 3
            for source in range(n_y):
                before = jnp.where(rising, front, total - front - depths[source])
                seen = jnp.exp(-before)
                image = [image[c] + got[source, view, c, tile] * seen for c in range(3)]
                front = front + depths[source]
            for c in range(3):
                img_ref[view, c, :, lanes] = image[c]
            tr_ref[view, :, lanes] = jnp.exp(-total)

    for other in range(n_y):
        @pl.when(other != iy)
        def _():
            share(other).wait_send()
    out_copy.wait()


def per_device(n_x, n_y, scalar_field, diffusivity, reaction_rate, shear_offsets, depth_order,
               tf_centres, tf_colour, tf_opacity):
    nx, ny, nz = scalar_field.shape
    views, bumps = depth_order.shape[0], tf_centres.shape[0]
    rows, ztiles = nx // n_y, nz // LANES
    f32 = jnp.float32
    vmem = pl.BlockSpec(memory_space=pltpu.VMEM)
    smem = pl.BlockSpec(memory_space=pltpu.SMEM)

    def space(*shape):
        return pltpu.VMEM(shape, f32)

    x_face, y_face = space(ny, nz), space(nx, nz)
    x_faces, y_faces = space(STEPS, ny, nz), space(STEPS, nx, nz)
    shares = space(n_y, views, 4, ztiles, rows, LANES)
    return pl.pallas_call(
        functools.partial(kernel, n_x, n_y),
        out_shape=(
            jax.ShapeDtypeStruct((nx, ny, nz), f32),
            jax.ShapeDtypeStruct((views, 3, rows, nz), f32),
            jax.ShapeDtypeStruct((views, rows, nz), f32),
        ),
        in_specs=[vmem, vmem, vmem, smem, vmem, smem, smem, smem],
        out_specs=(pl.BlockSpec(memory_space=pl.ANY), vmem, vmem),
        scratch_shapes=[
            space(2, nx, ny + SUB, nz), space(nx, ny + SUB, nz),
            x_faces, x_faces, x_face, x_face,
            y_faces, y_faces, y_faces, y_faces,
            y_face, y_face, y_face, y_face, y_face, y_face,
            space(ztiles + 1, ny * nx, LANES), space(ztiles + 1, ny * nx, LANES),
            shares, shares,
            space(views * ztiles, SUB, LANES), space(bumps, SUB, LANES),
            space(bumps, SUB, LANES), space(3, bumps, SUB, LANES),
            pltpu.SemaphoreType.DMA((STEPS + 1, 4)), pltpu.SemaphoreType.DMA((STEPS + 1, 4)),
            pltpu.SemaphoreType.DMA((n_y,)), pltpu.SemaphoreType.DMA((n_y,)),
            pltpu.SemaphoreType.DMA,
        ],
        compiler_params=pltpu.CompilerParams(
            collective_id=0, has_side_effects=True, vmem_limit_bytes=48 * 1024 * 1024),
    )(scalar_field, diffusivity, reaction_rate, shear_offsets, depth_order,
      tf_centres, tf_colour, tf_opacity)


def solution(mesh):
    grid = P("sx", "sy", None)
    return jax.shard_map(
        functools.partial(per_device, mesh.shape["sx"], mesh.shape["sy"]),
        mesh=mesh,
        in_specs=(grid, grid, grid, P(), P(), P(), P(), P()),
        out_specs=(grid, P(None, None, ("sx", "sy"), None), P(None, ("sx", "sy"), None)),
        check_vma=False,
    )
```

```python
import functools
import math

import jax
import jax.numpy as jnp
from jax import lax
from jax.experimental import pallas as pl
from jax.experimental.pallas import tpu as pltpu
from jax.sharding import PartitionSpec as P

STEPS = 4
DIFF_GAIN = 0.4
SHARPNESS = 2.0
LOG2E = math.log2(math.e)
SCALE = SHARPNESS * math.sqrt(LOG2E)
MESH = pl.DeviceIdType.MESH
LANES = 128
SUB = 8
UNROLL = 8
WIDE = 2


def conduct(diff, field):
    return diff * (1.0 + DIFF_GAIN * jnp.tanh(field))


def kernel(
    n_x, n_y,
    u_hbm, d_hbm, r_hbm, off_ref, ord_ref, cen_ref, col_ref, opa_ref,
    f_ref, img_ref, tr_ref,
    field, cond, x_lo, x_hi, dx_lo, dx_hi, p_lo, p_hi, y_lo, y_hi,
    dp_lo, dp_hi, dy_lo, dy_hi, del_lo, del_hi, tall, slope,
    part, got, sgn_ref, c2_ref, wop_ref, wcol_ref,
    d_ref, r_ref, halo_send, halo_recv, part_send, part_recv, out_sem, in_sem,
):
    nx, ny, nz = u_hbm.shape
    views = ord_ref.shape[0]
    bumps = cen_ref.shape[0]
    ztiles = nz // LANES
    rows = part.shape[4]
    per_group = SUB // rows
    groups = nx // SUB
    ix, iy = lax.axis_index("sx"), lax.axis_index("sy")

    fetches = [
        pltpu.make_async_copy(src, dst, in_sem.at[i]) for i, (src, dst) in enumerate((
            (u_hbm, field.at[0, :, pl.ds(0, ny)]), (d_hbm, d_ref), (r_hbm, r_ref)))
    ]
    for fetch in fetches:
        fetch.start()

    barrier = pltpu.get_barrier_semaphore()
    for hop in range(1, n_y):
        pl.semaphore_signal(
            barrier, inc=1, device_id={"sy": lax.rem(iy + hop, n_y)}, device_id_type=MESH)

    @pl.when(ix > 0)
    def _():
        pl.semaphore_signal(barrier, inc=1, device_id={"sx": ix - 1}, device_id_type=MESH)

    @pl.when(ix < n_x - 1)
    def _():
        pl.semaphore_signal(barrier, inc=1, device_id={"sx": ix + 1}, device_id_type=MESH)

    sides = [
        (ix > 0, {"sx": ix - 1}, 0, 1),
        (ix < n_x - 1, {"sx": ix + 1}, 1, 0),
        (iy > 0, {"sy": iy - 1}, 2, 3),
        (iy < n_y - 1, {"sy": iy + 1}, 3, 2),
    ]
    landings = [x_lo, x_hi, y_lo, y_hi]
    diff_landings = [dx_lo, dx_hi, dy_lo, dy_hi]

    def halo(step, side):
        exists, neighbour, here, there = sides[side]
        if step == STEPS:
            src = [d_ref.at[0], d_ref.at[nx - 1], dp_lo, dp_hi][side]
            dst, own = diff_landings[there], diff_landings[here]
        else:
            now = step % 2
            src = [
                field.at[now, 0, pl.ds(0, ny)], field.at[now, nx - 1, pl.ds(0, ny)],
                p_lo.at[step], p_hi.at[step],
            ][side]
            dst, own = landings[there].at[step], landings[here].at[step]
        go = pltpu.make_async_remote_copy(
            src_ref=src, dst_ref=dst, send_sem=halo_send.at[step, here],
            recv_sem=halo_recv.at[step, there], device_id=neighbour, device_id_type=MESH)
        come = pltpu.make_async_remote_copy(
            src_ref=src, dst_ref=own, send_sem=halo_send.at[step, here],
            recv_sem=halo_recv.at[step, here], device_id=neighbour, device_id_type=MESH)
        return exists, go, come

    def start_halos(step):
        for side in range(4):
            exists, go, _ = halo(step, side)
            pl.when(exists)(go.start)

    def wait_halos(step):
        for side in range(4):
            exists, go, come = halo(step, side)

            @pl.when(exists)
            def _():
                come.wait_recv()
                go.wait_send()

    for side in range(4):
        @pl.when(jnp.logical_not(sides[side][0]))
        def _():
            landings[side][...] = jnp.zeros_like(landings[side])
            diff_landings[side][...] = jnp.zeros_like(diff_landings[side])

    fetches[0].wait()
    fetches[1].wait()

    @pl.loop(0, groups)
    def _(block):
        base = pl.multiple_of(block * SUB, SUB)
        for ref, row, out in (
            (field.at[0], 0, p_lo.at[0]), (field.at[0], ny - 1, p_hi.at[0]),
            (d_ref, 0, dp_lo), (d_ref, ny - 1, dp_hi),
        ):
            out[pl.ds(base, SUB), :] = jnp.concatenate(
                [ref[base + j, row:row + 1, :] for j in range(SUB)], axis=0)

    arrivals = (n_y - 1) + (ix > 0).astype(jnp.int32) + (ix < n_x - 1).astype(jnp.int32)
    pl.semaphore_wait(barrier, arrivals)
    start_halos(0)
    start_halos(STEPS)

    row_at = lax.broadcasted_iota(jnp.int32, (SUB, nz), 0)
    col_at = lax.broadcasted_iota(jnp.int32, (SUB, nz), 1)

    for step in range(STEPS):
        now, later = step % 2, (step + 1) % 2

        @pl.loop(0, nx, unroll=4)
        def _(x):
            for t in range(ny // SUB):
                cut = pl.ds(t * SUB, SUB)
                cond[x, cut, :] = conduct(d_ref[x, cut, :], field[now, x, cut, :])

        if step == 0:
            fetches[2].wait()

        @pl.loop(0, nx, unroll=2)
        def _(x):
            below, above = jnp.maximum(x - 1, 0), jnp.minimum(x + 1, nx - 1)
            carried = None
            for t in range(ny // SUB):
                cut, shifted = pl.ds(t * SUB, SUB), pl.ds(t * SUB + 1, SUB)
                u, k = field[now, x, cut, :], cond[x, cut, :]
                change = (k + cond[below, cut, :]) * (field[now, below, cut, :] - u)
                change += (k + cond[above, cut, :]) * (field[now, above, cut, :] - u)
                flux = (k + cond[x, shifted, :]) * (field[now, x, shifted, :] - u)
                if t == ny // SUB - 1:
                    flux = jnp.where(row_at == SUB - 1, 0.0, flux)
                turned = pltpu.roll(flux, 1, 0)
                change += flux - jnp.where(row_at == 0, 0.0 if t == 0 else carried, turned)
                carried = turned
                ku = k * u
                right_u, right_k = pltpu.roll(u, nz - 1, 1), pltpu.roll(k, nz - 1, 1)
                flux = jnp.where(col_at == nz - 1, -ku, (k + right_k) * (right_u - u))
                change += flux - jnp.where(col_at == 0, ku, pltpu.roll(flux, 1, 1))
                field[later, x, cut, :] = u + 0.5 * change + r_ref[x, cut, :] * jnp.tanh(u)

        if step == 0:
            wait_halos(STEPS)
        wait_halos(step)
        inner = pl.ds(0, ny)
        for x, land, diff in ((0, x_lo, dx_lo), (nx - 1, x_hi, dx_hi)):
            beside = land[step]
            field[later, x, inner, :] += (
                0.5 * (cond[x, inner, :] + conduct(diff[...], beside))
                * (beside - field[now, x, inner, :]))
        for packed, own, land, diff, out in (
            (p_lo, dp_lo, y_lo, dy_lo, del_lo), (p_hi, dp_hi, y_hi, dy_hi, del_hi),
        ):
            u, beside = packed[step], land[step]
            out[...] = 0.5 * (conduct(own[...], u) + conduct(diff[...], beside)) * (beside - u)

        @pl.loop(0, groups)
        def _(block):
            base = pl.multiple_of(block * SUB, SUB)
            for packed, delta, row in ((p_lo, del_lo, 0), (p_hi, del_hi, ny - 1)):
                extra = delta[pl.ds(base, SUB), :]
                edge = []
                for j in range(SUB):
                    value = field[later, base + j, row:row + 1, :] + extra[j:j + 1, :]
                    field[later, base + j, row:row + 1, :] = value
                    edge.append(value)
                if step < STEPS - 1:
                    packed[step + 1, pl.ds(base, SUB), :] = jnp.concatenate(edge, axis=0)

        if step < STEPS - 1:
            start_halos(step + 1)

    last = STEPS % 2
    out_copy = pltpu.make_async_copy(field.at[last, :, pl.ds(0, ny)], f_ref, out_sem)
    out_copy.start()

    for ref in (tall, slope):
        ref[ztiles] = jnp.zeros_like(ref[ztiles])

    @pl.loop(0, nx, unroll=2)
    def _(x):
        for t in range(ny // SUB):
            value = field[last, x, pl.ds(t * SUB, SUB), :] * SCALE
            rise = jnp.where(col_at == nz - 1, 0.0, pltpu.roll(value, nz - 1, 1)) - value
            for tile in range(ztiles):
                lanes = slice(tile * LANES, (tile + 1) * LANES)
                spot = pl.ds(t * SUB * nx + x, SUB, stride=nx)
                tall[tile, spot, :] = value[:, lanes]
                slope[tile, spot, :] = rise[:, lanes]

    for view in range(views):
        for tile in range(ztiles):
            order = ord_ref[view:view + 1, tile * LANES:(tile + 1) * LANES]
            sign = jnp.where(order == 0, -1.0, 1.0)
            sgn_ref[view * ztiles + tile] = jnp.broadcast_to(sign, (SUB, LANES))
    for bump in range(bumps):
        centre = jnp.full((SUB, LANES), cen_ref[bump] * SCALE, jnp.float32)
        factor = jnp.exp2(-centre * centre)
        c2_ref[bump] = 2.0 * centre
        wop_ref[bump] = opa_ref[bump] * factor
        for channel in range(3):
            wcol_ref[channel, bump] = col_ref[channel, bump] * factor

    lane = lax.broadcasted_iota(jnp.int32, (SUB, LANES), 1)
    pairs = ztiles // WIDE

    def render(group, view, first):
        rate = [sgn_ref[view * ztiles + first + a] * LOG2E for a in range(WIDE)]

        def plane(y, carry):
            offset = off_ref[view, iy * ny + y]
            whole = offset >> 2
            frac = (offset & 3).astype(jnp.float32) * 0.25
            spot = pl.ds(pl.multiple_of(y * nx + group * SUB, SUB), SUB)
            turned = []
            for a in range(WIDE + 1):
                mixed = tall[first + a, spot, :] + frac * slope[first + a, spot, :]
                turned.append(pltpu.roll(mixed, (LANES - whole) & (LANES - 1), 1))
            inside = lane < LANES - whole
            result = []
            for a in range(WIDE):
                sums, depth, light = carry[a]
                s = jnp.where(inside, turned[a], turned[a + 1])
                bump = [jnp.exp2(s * (c2_ref[b] - s)) for b in range(bumps)]
                terms = [wop_ref[b] * bump[b] for b in range(bumps)]
                while len(terms) > 1:
                    terms = [i + j for i, j in zip(terms[::2], terms[1::2])]
                depth = depth + terms[0]
                new = jnp.exp2(rate[a] * depth)
                step = new - light
                sums = tuple(sums[b] + step * bump[b] for b in range(bumps))
                result.append((sums, depth, new))
            return tuple(result)

        def several(i, carry):
            for j in range(UNROLL):
                carry = plane(i * UNROLL + j, carry)
            return carry

        zero = jnp.zeros((SUB, LANES), jnp.float32)
        start = tuple(((zero,) * bumps, zero, zero + 1.0) for a in range(WIDE))
        ended = lax.fori_loop(0, ny // UNROLL, several, start)
        for a in range(WIDE):
            sums, depth, light = ended[a]
            sign = sgn_ref[view * ztiles + first + a]
            factor = jnp.where(sign > 0.0, jnp.exp(-depth), -1.0)
            values = []
            for channel in range(3):
                total = wcol_ref[channel, 0] * sums[0]
                for b in range(1, bumps):
                    total += wcol_ref[channel, b] * sums[b]
                values.append(total * factor)
            values.append(depth)
            for j in range(per_group):
                for channel, value in enumerate(values):
                    part[group * per_group + j, view, channel, first + a] = (
                        value[j * rows:(j + 1) * rows])

    def share(owner):
        return pltpu.make_async_remote_copy(
            src_ref=part.at[owner], dst_ref=got.at[iy], send_sem=part_send.at[owner],
            recv_sem=part_recv.at[iy], device_id={"sy": owner}, device_id_type=MESH)

    own_group = iy // per_group

    @pl.loop(0, groups)
    def _(turn):
        group = lax.rem(own_group + 1 + turn, groups)

        @pl.loop(0, views * pairs)
        def _(item):
            render(group, item // pairs, lax.rem(item, pairs) * WIDE)

        for j in range(per_group):
            owner = group * per_group + j

            @pl.when(owner != iy)
            def _():
                share(owner).start()

            @pl.when(owner == iy)
            def _():
                got[iy] = part[iy]

    for other in range(n_y):
        @pl.when(other != iy)
        def _():
            pltpu.make_async_remote_copy(
                src_ref=part.at[other], dst_ref=got.at[other], send_sem=part_send.at[other],
                recv_sem=part_recv.at[other], device_id={"sy": other}, device_id_type=MESH,
            ).wait_recv()

    for view in range(views):
        for tile in range(ztiles):
            lanes = slice(tile * LANES, (tile + 1) * LANES)
            rising = sgn_ref[view * ztiles + tile][:rows] < 0.0
            depths = [got[source, view, 3, tile] for source in range(n_y)]
            total = depths[0]
            for depth in depths[1:]:
                total = total + depth
            front = jnp.zeros_like(total)
            image = [jnp.zeros_like(total)] * 3
            for source in range(n_y):
                before = jnp.where(rising, front, total - front - depths[source])
                seen = jnp.exp(-before)
                image = [image[c] + got[source, view, c, tile] * seen for c in range(3)]
                front = front + depths[source]
            for c in range(3):
                img_ref[view, c, :, lanes] = image[c]
            tr_ref[view, :, lanes] = jnp.exp(-total)

    for other in range(n_y):
        @pl.when(other != iy)
        def _():
            share(other).wait_send()
    out_copy.wait()


def per_device(n_x, n_y, scalar_field, diffusivity, reaction_rate, shear_offsets, depth_order,
               tf_centres, tf_colour, tf_opacity):
    nx, ny, nz = scalar_field.shape
    views, bumps = depth_order.shape[0], tf_centres.shape[0]
    rows, ztiles = nx // n_y, nz // LANES
    f32 = jnp.float32
    vmem = pl.BlockSpec(memory_space=pltpu.VMEM)
    far = pl.BlockSpec(memory_space=pl.ANY)
    smem = pl.BlockSpec(memory_space=pltpu.SMEM)

    def space(*shape):
        return pltpu.VMEM(shape, f32)

    x_face, y_face = space(ny, nz), space(nx, nz)
    x_faces, y_faces = space(STEPS, ny, nz), space(STEPS, nx, nz)
    shares = space(n_y, views, 4, ztiles, rows, LANES)
    return pl.pallas_call(
        functools.partial(kernel, n_x, n_y),
        out_shape=(
            jax.ShapeDtypeStruct((nx, ny, nz), f32),
            jax.ShapeDtypeStruct((views, 3, rows, nz), f32),
            jax.ShapeDtypeStruct((views, rows, nz), f32),
        ),
        in_specs=[far, far, far, smem, vmem, smem, smem, smem],
        out_specs=(far, vmem, vmem),
        scratch_shapes=[
            space(2, nx, ny + SUB, nz), space(nx, ny + SUB, nz),
            x_faces, x_faces, x_face, x_face,
            y_faces, y_faces, y_faces, y_faces,
            y_face, y_face, y_face, y_face, y_face, y_face,
            space(ztiles + 1, ny * nx, LANES), space(ztiles + 1, ny * nx, LANES),
            shares, shares,
            space(views * ztiles, SUB, LANES), space(bumps, SUB, LANES),
            space(bumps, SUB, LANES), space(3, bumps, SUB, LANES),
            space(nx, ny, nz), space(nx, ny, nz),
            pltpu.SemaphoreType.DMA((STEPS + 1, 4)), pltpu.SemaphoreType.DMA((STEPS + 1, 4)),
            pltpu.SemaphoreType.DMA((n_y,)), pltpu.SemaphoreType.DMA((n_y,)),
            pltpu.SemaphoreType.DMA, pltpu.SemaphoreType.DMA((3,)),
        ],
        compiler_params=pltpu.CompilerParams(
            collective_id=0, has_side_effects=True, vmem_limit_bytes=60 * 1024 * 1024),
    )(scalar_field, diffusivity, reaction_rate, shear_offsets, depth_order,
      tf_centres, tf_colour, tf_opacity)


def solution(mesh):
    grid = P("sx", "sy", None)
    return jax.shard_map(
        functools.partial(per_device, mesh.shape["sx"], mesh.shape["sy"]),
        mesh=mesh,
        in_specs=(grid, grid, grid, P(), P(), P(), P(), P()),
        out_specs=(grid, P(None, None, ("sx", "sy"), None), P(None, ("sx", "sy"), None)),
        check_vma=False,
    )
```

```python
import functools
import math

import jax
import jax.numpy as jnp
from jax import lax
from jax.experimental import pallas as pl
from jax.experimental.pallas import tpu as pltpu
from jax.sharding import PartitionSpec as P

STEPS = 4
DIFF_GAIN = 0.4
SHARPNESS = 2.0
LOG2E = math.log2(math.e)
SCALE = SHARPNESS * math.sqrt(LOG2E)
MESH = pl.DeviceIdType.MESH
LANES = 128
SUB = 8
UNROLL = 16
WIDE = 2


def conduct(diff, field):
    return diff * (1.0 + DIFF_GAIN * jnp.tanh(field))


def kernel(
    n_x, n_y,
    u_hbm, d_hbm, r_hbm, off_hbm, ord_hbm, cen_hbm, col_hbm, opa_hbm,
    f_ref, img_ref, tr_ref,
    field, cond, x_lo, x_hi, dx_lo, dx_hi, p_lo, p_hi, y_lo, y_hi,
    dp_lo, dp_hi, dy_lo, dy_hi, del_lo, del_hi, tall, slope,
    part, mate, both, got, sgn_ref, c2_ref, wop_ref, wcol_ref,
    d_ref, r_ref, off_ref, ord_ref, cen_ref, col_ref, opa_ref,
    halo_send, halo_recv, mate_send, mate_recv, part_send, part_recv,
    out_sem, in_sem,
):
    nx, ny, nz = u_hbm.shape
    views = ord_ref.shape[0]
    bumps = cen_ref.shape[0]
    ztiles = nz // LANES
    rows = part.shape[4]
    per_group = SUB // rows
    groups = nx // SUB
    ix, iy = lax.axis_index("sx"), lax.axis_index("sy")

    fetches = [
        pltpu.make_async_copy(src, dst, in_sem.at[i]) for i, (src, dst) in enumerate((
            (u_hbm, field.at[0, :, pl.ds(0, ny)]), (d_hbm, d_ref), (r_hbm, r_ref),
            (off_hbm, off_ref), (ord_hbm, ord_ref), (cen_hbm, cen_ref), (col_hbm, col_ref),
            (opa_hbm, opa_ref)))
    ]
    for fetch in fetches:
        fetch.start()

    barrier = pltpu.get_barrier_semaphore()
    for hop in range(1, n_y):
        pl.semaphore_signal(
            barrier, inc=1, device_id={"sy": lax.rem(iy + hop, n_y)}, device_id_type=MESH)

    @pl.when(ix > 0)
    def _():
        pl.semaphore_signal(barrier, inc=1, device_id={"sx": ix - 1}, device_id_type=MESH)

    @pl.when(ix < n_x - 1)
    def _():
        pl.semaphore_signal(barrier, inc=1, device_id={"sx": ix + 1}, device_id_type=MESH)

    sides = [
        (ix > 0, {"sx": ix - 1}, 0, 1),
        (ix < n_x - 1, {"sx": ix + 1}, 1, 0),
        (iy > 0, {"sy": iy - 1}, 2, 3),
        (iy < n_y - 1, {"sy": iy + 1}, 3, 2),
    ]
    landings = [x_lo, x_hi, y_lo, y_hi]
    diff_landings = [dx_lo, dx_hi, dy_lo, dy_hi]

    def halo(step, side):
        exists, neighbour, here, there = sides[side]
        if step == STEPS:
            src = [d_ref.at[0], d_ref.at[nx - 1], dp_lo, dp_hi][side]
            dst, own = diff_landings[there], diff_landings[here]
        else:
            now = step % 2
            src = [
                field.at[now, 0, pl.ds(0, ny)], field.at[now, nx - 1, pl.ds(0, ny)],
                p_lo.at[step], p_hi.at[step],
            ][side]
            dst, own = landings[there].at[step], landings[here].at[step]
        go = pltpu.make_async_remote_copy(
            src_ref=src, dst_ref=dst, send_sem=halo_send.at[step, here],
            recv_sem=halo_recv.at[step, there], device_id=neighbour, device_id_type=MESH)
        come = pltpu.make_async_remote_copy(
            src_ref=src, dst_ref=own, send_sem=halo_send.at[step, here],
            recv_sem=halo_recv.at[step, here], device_id=neighbour, device_id_type=MESH)
        return exists, go, come

    def start_halos(step):
        for side in range(4):
            exists, go, _ = halo(step, side)
            pl.when(exists)(go.start)

    def wait_halos(step):
        for side in range(4):
            exists, go, come = halo(step, side)

            @pl.when(exists)
            def _():
                come.wait_recv()
                go.wait_send()

    for side in range(4):
        @pl.when(jnp.logical_not(sides[side][0]))
        def _():
            landings[side][...] = jnp.zeros_like(landings[side])
            diff_landings[side][...] = jnp.zeros_like(diff_landings[side])

    fetches[0].wait()
    fetches[1].wait()

    @pl.loop(0, groups, unroll=True)
    def _(block):
        base = pl.multiple_of(block * SUB, SUB)
        for ref, row, out in (
            (field.at[0], 0, p_lo.at[0]), (field.at[0], ny - 1, p_hi.at[0]),
            (d_ref, 0, dp_lo), (d_ref, ny - 1, dp_hi),
        ):
            out[pl.ds(base, SUB), :] = jnp.concatenate(
                [ref[base + j, row:row + 1, :] for j in range(SUB)], axis=0)

    arrivals = (n_y - 1) + (ix > 0).astype(jnp.int32) + (ix < n_x - 1).astype(jnp.int32)
    pl.semaphore_wait(barrier, arrivals)
    start_halos(0)
    start_halos(STEPS)

    row_at = lax.broadcasted_iota(jnp.int32, (SUB, nz), 0)
    col_at = lax.broadcasted_iota(jnp.int32, (SUB, nz), 1)

    for step in range(STEPS):
        now, later = step % 2, (step + 1) % 2

        @pl.loop(0, nx, unroll=8)
        def _(x):
            for t in range(ny // SUB):
                cut = pl.ds(t * SUB, SUB)
                cond[x, cut, :] = conduct(d_ref[x, cut, :], field[now, x, cut, :])

        if step == 0:
            fetches[2].wait()

        @pl.loop(0, nx, unroll=4)
        def _(x):
            below, above = jnp.maximum(x - 1, 0), jnp.minimum(x + 1, nx - 1)
            tiles = ny // SUB
            cuts = [pl.ds(t * SUB, SUB) for t in range(tiles)]
            us = [field[now, x, cut, :] for cut in cuts]
            ks = [cond[x, cut, :] for cut in cuts]
            up_u = [pltpu.roll(u, SUB - 1, 0) for u in us]
            up_k = [pltpu.roll(k, SUB - 1, 0) for k in ks]
            carried = None
            for t, cut in enumerate(cuts):
                u, k = us[t], ks[t]
                change = (k + cond[below, cut, :]) * (field[now, below, cut, :] - u)
                change += (k + cond[above, cut, :]) * (field[now, above, cut, :] - u)
                if t < tiles - 1:
                    next_u = jnp.where(row_at == SUB - 1, up_u[t + 1], up_u[t])
                    next_k = jnp.where(row_at == SUB - 1, up_k[t + 1], up_k[t])
                else:
                    next_u, next_k = up_u[t], up_k[t]
                flux = (k + next_k) * (next_u - u)
                if t == tiles - 1:
                    flux = jnp.where(row_at == SUB - 1, 0.0, flux)
                turned = pltpu.roll(flux, 1, 0)
                change += flux - jnp.where(row_at == 0, 0.0 if t == 0 else carried, turned)
                carried = turned
                ku = k * u
                right_u, right_k = pltpu.roll(u, nz - 1, 1), pltpu.roll(k, nz - 1, 1)
                flux = jnp.where(col_at == nz - 1, -ku, (k + right_k) * (right_u - u))
                change += flux - jnp.where(col_at == 0, ku, pltpu.roll(flux, 1, 1))
                field[later, x, cut, :] = u + 0.5 * change + r_ref[x, cut, :] * jnp.tanh(u)

        if step == 0:
            wait_halos(STEPS)
        wait_halos(step)
        inner = pl.ds(0, ny)
        for x, land, diff in ((0, x_lo, dx_lo), (nx - 1, x_hi, dx_hi)):
            beside = land[step]
            field[later, x, inner, :] += (
                0.5 * (cond[x, inner, :] + conduct(diff[...], beside))
                * (beside - field[now, x, inner, :]))
        for packed, own, land, diff, out in (
            (p_lo, dp_lo, y_lo, dy_lo, del_lo), (p_hi, dp_hi, y_hi, dy_hi, del_hi),
        ):
            u, beside = packed[step], land[step]
            out[...] = 0.5 * (conduct(own[...], u) + conduct(diff[...], beside)) * (beside - u)

        @pl.loop(0, groups, unroll=True)
        def _(block):
            base = pl.multiple_of(block * SUB, SUB)
            for packed, delta, row in ((p_lo, del_lo, 0), (p_hi, del_hi, ny - 1)):
                extra = delta[pl.ds(base, SUB), :]
                edge = []
                for j in range(SUB):
                    value = field[later, base + j, row:row + 1, :] + extra[j:j + 1, :]
                    field[later, base + j, row:row + 1, :] = value
                    edge.append(value)
                if step < STEPS - 1:
                    packed[step + 1, pl.ds(base, SUB), :] = jnp.concatenate(edge, axis=0)

        if step < STEPS - 1:
            start_halos(step + 1)

    last = STEPS % 2
    out_copy = pltpu.make_async_copy(field.at[last, :, pl.ds(0, ny)], f_ref, out_sem)
    out_copy.start()

    for ref in (tall, slope):
        ref[ztiles] = jnp.zeros_like(ref[ztiles])

    @pl.loop(0, nx, unroll=2)
    def _(x):
        for t in range(ny // SUB):
            value = field[last, x, pl.ds(t * SUB, SUB), :] * SCALE
            rise = jnp.where(col_at == nz - 1, 0.0, pltpu.roll(value, nz - 1, 1)) - value
            for tile in range(ztiles):
                lanes = slice(tile * LANES, (tile + 1) * LANES)
                spot = pl.ds(t * SUB * nx + x, SUB, stride=nx)
                tall[tile, spot, :] = value[:, lanes]
                slope[tile, spot, :] = rise[:, lanes]

    for fetch in fetches[3:]:
        fetch.wait()
    for view in range(views):
        for tile in range(ztiles):
            order = ord_ref[view:view + 1, tile * LANES:(tile + 1) * LANES]
            sign = jnp.where(order == 0, -1.0, 1.0)
            sgn_ref[view * ztiles + tile] = jnp.broadcast_to(sign, (SUB, LANES))
    for bump in range(bumps):
        centre = jnp.full((SUB, LANES), cen_ref[bump] * SCALE, jnp.float32)
        factor = jnp.exp2(-centre * centre)
        c2_ref[bump] = 2.0 * centre
        wop_ref[bump] = opa_ref[bump] * factor
        for channel in range(3):
            wcol_ref[channel, bump] = col_ref[channel, bump] * factor

    lane = lax.broadcasted_iota(jnp.int32, (SUB, LANES), 1)
    pairs = ztiles // WIDE

    def render(group, view, first):
        rate = [sgn_ref[view * ztiles + first + a] * LOG2E for a in range(WIDE)]

        def plane(y, carry):
            offset = off_ref[view, iy * ny + y]
            whole = offset >> 2
            frac = (offset & 3).astype(jnp.float32) * 0.25
            spot = pl.ds(pl.multiple_of(y * nx + group * SUB, SUB), SUB)
            turned = []
            for a in range(WIDE + 1):
                mixed = tall[first + a, spot, :] + frac * slope[first + a, spot, :]
                turned.append(pltpu.roll(mixed, (LANES - whole) & (LANES - 1), 1))
            inside = lane < LANES - whole
            result = []
            for a in range(WIDE):
                sums, depth, light = carry[a]
                s = jnp.where(inside, turned[a], turned[a + 1])
                bump = [jnp.exp2(s * (c2_ref[b] - s)) for b in range(bumps)]
                terms = [wop_ref[b] * bump[b] for b in range(bumps)]
                while len(terms) > 1:
                    terms = [i + j for i, j in zip(terms[::2], terms[1::2])]
                depth = depth + terms[0]
                new = jnp.exp2(rate[a] * depth)
                step = new - light
                sums = tuple(sums[b] + step * bump[b] for b in range(bumps))
                result.append((sums, depth, new))
            return tuple(result)

        def several(i, carry):
            for j in range(UNROLL):
                carry = plane(i * UNROLL + j, carry)
            return carry

        zero = jnp.zeros((SUB, LANES), jnp.float32)
        start = tuple(((zero,) * bumps, zero, zero + 1.0) for a in range(WIDE))
        ended = lax.fori_loop(0, ny // UNROLL, several, start)
        for a in range(WIDE):
            sums, depth, light = ended[a]
            sign = sgn_ref[view * ztiles + first + a]
            factor = jnp.where(sign > 0.0, jnp.exp(-depth), -1.0)
            values = []
            for channel in range(3):
                total = wcol_ref[channel, 0] * sums[0]
                for b in range(1, bumps):
                    total += wcol_ref[channel, b] * sums[b]
                values.append(total * factor)
            values.append(depth)
            for j in range(per_group):
                for channel, value in enumerate(values):
                    part[group * per_group + j, view, channel, first + a] = (
                        value[j * rows:(j + 1) * rows])

    core, pair = lax.rem(iy, 2), iy // 2
    twin = iy + 1 - 2 * core
    group_pairs = per_group // 2
    flip = (1 - 2 * core).astype(jnp.float32)

    def hand(which):
        return pltpu.make_async_remote_copy(
            src_ref=part.at[2 * which + 1 - core], dst_ref=mate.at[which],
            send_sem=mate_send.at[which], recv_sem=mate_recv.at[which],
            device_id={"sy": twin}, device_id_type=MESH)

    def share(which, slot):
        return pltpu.make_async_remote_copy(
            src_ref=both.at[which], dst_ref=got.at[slot], send_sem=part_send.at[which],
            recv_sem=part_recv.at[slot], device_id={"sy": 2 * which + core}, device_id_type=MESH)

    def merge(which):
        hand(which).wait_recv()
        for view in range(views):
            for tile in range(ztiles):
                mine_first = sgn_ref[view * ztiles + tile][:rows] * flip < 0.0
                mine = [part[2 * which + core, view, c, tile] for c in range(4)]
                other = [mate[which, view, c, tile] for c in range(4)]
                dim = jnp.exp(-jnp.where(mine_first, mine[3], other[3]))
                for c in range(3):
                    near = jnp.where(mine_first, mine[c], other[c])
                    far = jnp.where(mine_first, other[c], mine[c])
                    both[which, view, c, tile] = near + dim * far
                both[which, view, 3, tile] = mine[3] + other[3]

    def finish(group):
        for j in range(group_pairs):
            which = group * group_pairs + j
            merge(which)

            @pl.when(which != pair)
            def _():
                share(which, pair).start()

            @pl.when(which == pair)
            def _():
                got[pair] = both[pair]

    own_group = iy // per_group
    early = min(2, views * pairs)

    @pl.loop(0, groups)
    def _(turn):
        group = lax.rem(own_group + 1 + turn, groups)

        def item_at(item):
            render(group, item // pairs, lax.rem(item, pairs) * WIDE)

        pl.loop(0, early)(item_at)

        @pl.when(turn > 0)
        def _():
            finish(lax.rem(own_group + turn, groups))

        pl.loop(early, views * pairs)(item_at)
        for j in range(group_pairs):
            hand(group * group_pairs + j).start()

    finish(own_group)
    for other in range(n_y // 2):
        @pl.when(other != pair)
        def _():
            share(other, other).wait_recv()

    for view in range(views):
        for tile in range(ztiles):
            lanes = slice(tile * LANES, (tile + 1) * LANES)
            rising = sgn_ref[view * ztiles + tile][:rows] < 0.0
            depths = [got[source, view, 3, tile] for source in range(n_y // 2)]
            total = depths[0]
            for depth in depths[1:]:
                total = total + depth
            front = jnp.zeros_like(total)
            image = [jnp.zeros_like(total)] * 3
            for source in range(n_y // 2):
                before = jnp.where(rising, front, total - front - depths[source])
                seen = jnp.exp(-before)
                image = [image[c] + got[source, view, c, tile] * seen for c in range(3)]
                front = front + depths[source]
            for c in range(3):
                img_ref[view, c, :, lanes] = image[c]
            tr_ref[view, :, lanes] = jnp.exp(-total)

    for other in range(n_y // 2):
        hand(other).wait_send()

        @pl.when(other != pair)
        def _():
            share(other, pair).wait_send()
    out_copy.wait()


def per_device(n_x, n_y, scalar_field, diffusivity, reaction_rate, shear_offsets, depth_order,
               tf_centres, tf_colour, tf_opacity):
    nx, ny, nz = scalar_field.shape
    views, bumps = depth_order.shape[0], tf_centres.shape[0]
    rows, ztiles = nx // n_y, nz // LANES
    f32 = jnp.float32
    vmem = pl.BlockSpec(memory_space=pltpu.VMEM)
    far = pl.BlockSpec(memory_space=pl.ANY)
    pinned = pl.BlockSpec(memory_space=pltpu.HBM)

    def space(*shape):
        return pltpu.VMEM(shape, f32)

    x_face, y_face = space(ny, nz), space(nx, nz)
    x_faces, y_faces = space(STEPS, ny, nz), space(STEPS, nx, nz)
    shares = space(n_y, views, 4, ztiles, rows, LANES)
    halves = space(n_y // 2, views, 4, ztiles, rows, LANES)
    return pl.pallas_call(
        functools.partial(kernel, n_x, n_y),
        out_shape=(
            jax.ShapeDtypeStruct((nx, ny, nz), f32),
            jax.ShapeDtypeStruct((views, 3, rows, nz), f32),
            jax.ShapeDtypeStruct((views, rows, nz), f32),
        ),
        in_specs=[pinned] * 8,
        out_specs=(far, vmem, vmem),
        scratch_shapes=[
            space(2, nx, ny + SUB, nz), space(nx, ny + SUB, nz),
            x_faces, x_faces, x_face, x_face,
            y_faces, y_faces, y_faces, y_faces,
            y_face, y_face, y_face, y_face, y_face, y_face,
            space(ztiles + 1, ny * nx, LANES), space(ztiles + 1, ny * nx, LANES),
            shares, halves, halves, halves,
            space(views * ztiles, SUB, LANES), space(bumps, SUB, LANES),
            space(bumps, SUB, LANES), space(3, bumps, SUB, LANES),
            space(nx, ny, nz), space(nx, ny, nz),
            pltpu.SMEM(shear_offsets.shape, jnp.int32), pltpu.VMEM(depth_order.shape, jnp.int32),
            pltpu.SMEM(tf_centres.shape, f32), pltpu.SMEM(tf_colour.shape, f32),
            pltpu.SMEM(tf_opacity.shape, f32),
            pltpu.SemaphoreType.DMA((STEPS + 1, 4)), pltpu.SemaphoreType.DMA((STEPS + 1, 4)),
            *[pltpu.SemaphoreType.DMA((n_y // 2,))] * 4,
            pltpu.SemaphoreType.DMA, pltpu.SemaphoreType.DMA((8,)),
        ],
        compiler_params=pltpu.CompilerParams(
            collective_id=0, has_side_effects=True, vmem_limit_bytes=60 * 1024 * 1024),
    )(scalar_field, diffusivity, reaction_rate, shear_offsets, depth_order,
      tf_centres, tf_colour, tf_opacity)


def solution(mesh):
    grid = P("sx", "sy", None)
    return jax.shard_map(
        functools.partial(per_device, mesh.shape["sx"], mesh.shape["sy"]),
        mesh=mesh,
        in_specs=(grid, grid, grid, P(), P(), P(), P(), P()),
        out_specs=(grid, P(None, None, ("sx", "sy"), None), P(None, ("sx", "sy"), None)),
        check_vma=False,
    )
```

```python
import functools
import math

import jax
import jax.numpy as jnp
from jax import lax
from jax.experimental import pallas as pl
from jax.experimental.pallas import tpu as pltpu
from jax.sharding import PartitionSpec as P

STEPS = 4
DIFF_GAIN = 0.4
SHARPNESS = 2.0
LOG2E = math.log2(math.e)
SCALE = SHARPNESS * math.sqrt(LOG2E)
MESH = pl.DeviceIdType.MESH
LANES = 128
SUB = 8
UNROLL = 32
CHUNKS = 8
WIDE = 2


def conduct(diff, field):
    return diff * (1.0 + DIFF_GAIN * jnp.tanh(field))


def kernel(
    n_x, n_y,
    u_hbm, d_hbm, r_hbm, off_hbm, ord_hbm, cen_hbm, col_hbm, opa_hbm,
    f_ref, img_ref, tr_ref,
    field, cond, x_lo, x_hi, dx_lo, dx_hi, p_lo, p_hi, y_lo, y_hi,
    dp_lo, dp_hi, dy_lo, dy_hi, del_lo, del_hi, tall, slope,
    part, mate, both, got, sgn_ref, c2_ref, wop_ref, wcol_ref,
    d_ref, r_ref, off_ref, ord_ref, cen_ref, col_ref, opa_ref,
    halo_send, halo_recv, mate_send, mate_recv, part_send, part_recv,
    out_sem, in_sem,
):
    nx, ny, nz = u_hbm.shape
    views = ord_ref.shape[0]
    bumps = cen_ref.shape[0]
    ztiles = nz // LANES
    rows = part.shape[4]
    per_group = SUB // rows
    groups = nx // SUB
    ix, iy = lax.axis_index("sx"), lax.axis_index("sy")

    fetches = [
        pltpu.make_async_copy(src, dst, in_sem.at[i]) for i, (src, dst) in enumerate((
            (u_hbm, field.at[0, :, pl.ds(0, ny)]), (d_hbm, d_ref), (r_hbm, r_ref),
            (off_hbm, off_ref), (ord_hbm, ord_ref), (cen_hbm, cen_ref), (col_hbm, col_ref),
            (opa_hbm, opa_ref)))
    ]
    for fetch in fetches:
        fetch.start()

    barrier = pltpu.get_barrier_semaphore()
    for hop in range(1, n_y):
        pl.semaphore_signal(
            barrier, inc=1, device_id={"sy": lax.rem(iy + hop, n_y)}, device_id_type=MESH)

    @pl.when(ix > 0)
    def _():
        pl.semaphore_signal(barrier, inc=1, device_id={"sx": ix - 1}, device_id_type=MESH)

    @pl.when(ix < n_x - 1)
    def _():
        pl.semaphore_signal(barrier, inc=1, device_id={"sx": ix + 1}, device_id_type=MESH)

    sides = [
        (ix > 0, {"sx": ix - 1}, 0, 1),
        (ix < n_x - 1, {"sx": ix + 1}, 1, 0),
        (iy > 0, {"sy": iy - 1}, 2, 3),
        (iy < n_y - 1, {"sy": iy + 1}, 3, 2),
    ]
    landings = [x_lo, x_hi, y_lo, y_hi]
    diff_landings = [dx_lo, dx_hi, dy_lo, dy_hi]

    def halo(step, side):
        exists, neighbour, here, there = sides[side]
        if step == STEPS:
            src = [d_ref.at[0], d_ref.at[nx - 1], dp_lo, dp_hi][side]
            dst, own = diff_landings[there], diff_landings[here]
        else:
            now = step % 2
            src = [
                field.at[now, 0, pl.ds(0, ny)], field.at[now, nx - 1, pl.ds(0, ny)],
                p_lo.at[step], p_hi.at[step],
            ][side]
            dst, own = landings[there].at[step], landings[here].at[step]
        go = pltpu.make_async_remote_copy(
            src_ref=src, dst_ref=dst, send_sem=halo_send.at[step, here],
            recv_sem=halo_recv.at[step, there], device_id=neighbour, device_id_type=MESH)
        come = pltpu.make_async_remote_copy(
            src_ref=src, dst_ref=own, send_sem=halo_send.at[step, here],
            recv_sem=halo_recv.at[step, here], device_id=neighbour, device_id_type=MESH)
        return exists, go, come

    def start_halos(step):
        for side in range(4):
            exists, go, _ = halo(step, side)
            pl.when(exists)(go.start)

    def wait_halos(step):
        for side in range(4):
            exists, go, come = halo(step, side)

            @pl.when(exists)
            def _():
                come.wait_recv()
                go.wait_send()

    for side in range(4):
        @pl.when(jnp.logical_not(sides[side][0]))
        def _():
            landings[side][...] = jnp.zeros_like(landings[side])
            diff_landings[side][...] = jnp.zeros_like(diff_landings[side])

    fetches[0].wait()
    fetches[1].wait()

    @pl.loop(0, groups, unroll=True)
    def _(block):
        base = pl.multiple_of(block * SUB, SUB)
        for ref, row, out in (
            (field.at[0], 0, p_lo.at[0]), (field.at[0], ny - 1, p_hi.at[0]),
            (d_ref, 0, dp_lo), (d_ref, ny - 1, dp_hi),
        ):
            out[pl.ds(base, SUB), :] = jnp.concatenate(
                [ref[base + j, row:row + 1, :] for j in range(SUB)], axis=0)

    arrivals = (n_y - 1) + (ix > 0).astype(jnp.int32) + (ix < n_x - 1).astype(jnp.int32)
    pl.semaphore_wait(barrier, arrivals)
    start_halos(0)
    start_halos(STEPS)

    row_at = lax.broadcasted_iota(jnp.int32, (SUB, nz), 0)
    col_at = lax.broadcasted_iota(jnp.int32, (SUB, nz), 1)

    for step in range(STEPS):
        now, later = step % 2, (step + 1) % 2

        @pl.loop(0, nx, unroll=8)
        def _(x):
            for t in range(ny // SUB):
                cut = pl.ds(t * SUB, SUB)
                cond[x, cut, :] = conduct(d_ref[x, cut, :], field[now, x, cut, :])

        if step == 0:
            fetches[2].wait()

        @pl.loop(0, nx, unroll=4)
        def _(x):
            below, above = jnp.maximum(x - 1, 0), jnp.minimum(x + 1, nx - 1)
            tiles = ny // SUB
            cuts = [pl.ds(t * SUB, SUB) for t in range(tiles)]
            us = [field[now, x, cut, :] for cut in cuts]
            ks = [cond[x, cut, :] for cut in cuts]
            up_u = [pltpu.roll(u, SUB - 1, 0) for u in us]
            up_k = [pltpu.roll(k, SUB - 1, 0) for k in ks]
            carried = None
            for t, cut in enumerate(cuts):
                u, k = us[t], ks[t]
                change = (k + cond[below, cut, :]) * (field[now, below, cut, :] - u)
                change += (k + cond[above, cut, :]) * (field[now, above, cut, :] - u)
                if t < tiles - 1:
                    next_u = jnp.where(row_at == SUB - 1, up_u[t + 1], up_u[t])
                    next_k = jnp.where(row_at == SUB - 1, up_k[t + 1], up_k[t])
                else:
                    next_u, next_k = up_u[t], up_k[t]
                flux = (k + next_k) * (next_u - u)
                if t == tiles - 1:
                    flux = jnp.where(row_at == SUB - 1, 0.0, flux)
                turned = pltpu.roll(flux, 1, 0)
                change += flux - jnp.where(row_at == 0, 0.0 if t == 0 else carried, turned)
                carried = turned
                ku = k * u
                right_u, right_k = pltpu.roll(u, nz - 1, 1), pltpu.roll(k, nz - 1, 1)
                flux = jnp.where(col_at == nz - 1, -ku, (k + right_k) * (right_u - u))
                change += flux - jnp.where(col_at == 0, ku, pltpu.roll(flux, 1, 1))
                field[later, x, cut, :] = u + 0.5 * change + r_ref[x, cut, :] * jnp.tanh(u)

        if step == 0:
            wait_halos(STEPS)
        wait_halos(step)
        inner = pl.ds(0, ny)
        for x, land, diff in ((0, x_lo, dx_lo), (nx - 1, x_hi, dx_hi)):
            beside = land[step]
            field[later, x, inner, :] += (
                0.5 * (cond[x, inner, :] + conduct(diff[...], beside))
                * (beside - field[now, x, inner, :]))
        for packed, own, land, diff, out in (
            (p_lo, dp_lo, y_lo, dy_lo, del_lo), (p_hi, dp_hi, y_hi, dy_hi, del_hi),
        ):
            u, beside = packed[step], land[step]
            out[...] = 0.5 * (conduct(own[...], u) + conduct(diff[...], beside)) * (beside - u)

        @pl.loop(0, groups, unroll=True)
        def _(block):
            base = pl.multiple_of(block * SUB, SUB)
            for packed, delta, row in ((p_lo, del_lo, 0), (p_hi, del_hi, ny - 1)):
                extra = delta[pl.ds(base, SUB), :]
                edge = []
                for j in range(SUB):
                    value = field[later, base + j, row:row + 1, :] + extra[j:j + 1, :]
                    field[later, base + j, row:row + 1, :] = value
                    edge.append(value)
                if step < STEPS - 1:
                    packed[step + 1, pl.ds(base, SUB), :] = jnp.concatenate(edge, axis=0)

        if step < STEPS - 1:
            start_halos(step + 1)

    last = STEPS % 2
    out_copy = pltpu.make_async_copy(field.at[last, :, pl.ds(0, ny)], f_ref, out_sem)
    out_copy.start()

    for ref in (tall, slope):
        ref[ztiles] = jnp.zeros_like(ref[ztiles])

    @pl.loop(0, nx, unroll=2)
    def _(x):
        for t in range(ny // SUB):
            value = field[last, x, pl.ds(t * SUB, SUB), :] * SCALE
            for tile in range(ztiles):
                spot = pl.ds(t * SUB * nx + x, SUB, stride=nx)
                tall[tile, spot, :] = value[:, tile * LANES:(tile + 1) * LANES]

    lane = lax.broadcasted_iota(jnp.int32, (SUB, LANES), 1)

    @pl.loop(0, ny * nx // SUB, unroll=4)
    def _(block):
        spot = pl.ds(pl.multiple_of(block * SUB, SUB), SUB)
        values = [tall[tile, spot, :] for tile in range(ztiles)]
        ahead = [pltpu.roll(value, LANES - 1, 1) for value in values] + [0.0]
        for tile in range(ztiles):
            beside = jnp.where(lane == LANES - 1, ahead[tile + 1], ahead[tile])
            slope[tile, spot, :] = beside - values[tile]

    for fetch in fetches[3:]:
        fetch.wait()
    for view in range(views):
        for tile in range(ztiles):
            order = ord_ref[view:view + 1, tile * LANES:(tile + 1) * LANES]
            sign = jnp.where(order == 0, -1.0, 1.0)
            sgn_ref[view * ztiles + tile] = jnp.broadcast_to(sign, (SUB, LANES))
    for bump in range(bumps):
        centre = jnp.full((SUB, LANES), cen_ref[bump] * SCALE, jnp.float32)
        factor = jnp.exp2(-centre * centre)
        c2_ref[bump] = 2.0 * centre
        wop_ref[bump] = opa_ref[bump] * factor
        for channel in range(3):
            wcol_ref[channel, bump] = col_ref[channel, bump] * factor

    pairs = ztiles // WIDE

    def render(group, view, first):
        rate = [sgn_ref[view * ztiles + first + a] * LOG2E for a in range(WIDE)]

        def plane(y, carry):
            offset = off_ref[view, iy * ny + y]
            whole = offset >> 2
            frac = (offset & 3).astype(jnp.float32) * 0.25
            spot = pl.ds(pl.multiple_of(y * nx + group * SUB, SUB), SUB)
            turned = []
            for a in range(WIDE + 1):
                mixed = tall[first + a, spot, :] + frac * slope[first + a, spot, :]
                turned.append(pltpu.roll(mixed, (LANES - whole) & (LANES - 1), 1))
            inside = lane < LANES - whole
            result = []
            for a in range(WIDE):
                sums, depth, light = carry[a]
                s = jnp.where(inside, turned[a], turned[a + 1])
                bump = [jnp.exp2(s * (c2_ref[b] - s)) for b in range(bumps)]
                terms = [wop_ref[b] * bump[b] for b in range(bumps)]
                while len(terms) > 1:
                    terms = [i + j for i, j in zip(terms[::2], terms[1::2])]
                depth = depth + terms[0]
                new = jnp.exp2(rate[a] * depth)
                step = new - light
                sums = tuple(sums[b] + step * bump[b] for b in range(bumps))
                result.append((sums, depth, new))
            return tuple(result)

        unroll = min(UNROLL, ny)

        def several(i, carry):
            for j in range(unroll):
                carry = plane(i * unroll + j, carry)
            return carry

        zero = jnp.zeros((SUB, LANES), jnp.float32)
        start = tuple(((zero,) * bumps, zero, zero + 1.0) for a in range(WIDE))
        ended = lax.fori_loop(0, ny // unroll, several, start)
        for a in range(WIDE):
            sums, depth, light = ended[a]
            sign = sgn_ref[view * ztiles + first + a]
            factor = jnp.where(sign > 0.0, jnp.exp(-depth), -1.0)
            values = []
            for channel in range(3):
                total = wcol_ref[channel, 0] * sums[0]
                for b in range(1, bumps):
                    total += wcol_ref[channel, b] * sums[b]
                values.append(total * factor)
            values.append(depth)
            for j in range(per_group):
                for channel, value in enumerate(values):
                    part[group * per_group + j, view, channel, first + a] = (
                        value[j * rows:(j + 1) * rows])

    core, pair = lax.rem(iy, 2), iy // 2
    twin = iy + 1 - 2 * core
    group_pairs = per_group // 2
    flip = (1 - 2 * core).astype(jnp.float32)

    def hand(which):
        return pltpu.make_async_remote_copy(
            src_ref=part.at[2 * which + 1 - core], dst_ref=mate.at[which],
            send_sem=mate_send.at[which], recv_sem=mate_recv.at[which],
            device_id={"sy": twin}, device_id_type=MESH)

    def share(which, slot):
        return pltpu.make_async_remote_copy(
            src_ref=both.at[which], dst_ref=got.at[slot], send_sem=part_send.at[which],
            recv_sem=part_recv.at[slot], device_id={"sy": 2 * which + core}, device_id_type=MESH)

    def merge(which):
        hand(which).wait_recv()
        for view in range(views):
            for tile in range(ztiles):
                mine_first = sgn_ref[view * ztiles + tile][:rows] * flip < 0.0
                mine = [part[2 * which + core, view, c, tile] for c in range(4)]
                other = [mate[which, view, c, tile] for c in range(4)]
                dim = jnp.exp(-jnp.where(mine_first, mine[3], other[3]))
                for c in range(3):
                    near = jnp.where(mine_first, mine[c], other[c])
                    far = jnp.where(mine_first, other[c], mine[c])
                    both[which, view, c, tile] = near + dim * far
                both[which, view, 3, tile] = mine[3] + other[3]

    def finish(group):
        for j in range(group_pairs):
            which = group * group_pairs + j
            merge(which)

            @pl.when(which != pair)
            def _():
                share(which, pair).start()

            @pl.when(which == pair)
            def _():
                got[pair] = both[pair]

    own_group = iy // per_group
    early = min(2, views * pairs)

    @pl.loop(0, groups)
    def _(turn):
        group = lax.rem(own_group + 1 + turn, groups)

        def item_at(item):
            render(group, item // pairs, lax.rem(item, pairs) * WIDE)

        pl.loop(0, early)(item_at)

        @pl.when(turn > 0)
        def _():
            finish(lax.rem(own_group + turn, groups))

        pl.loop(early, views * pairs)(item_at)
        for j in range(group_pairs):
            hand(group * group_pairs + j).start()

    finish(own_group)
    for other in range(n_y // 2):
        @pl.when(other != pair)
        def _():
            share(other, other).wait_recv()

    for view in range(views):
        for tile in range(ztiles):
            lanes = slice(tile * LANES, (tile + 1) * LANES)
            rising = sgn_ref[view * ztiles + tile][:rows] < 0.0
            depths = [got[source, view, 3, tile] for source in range(n_y // 2)]
            total = depths[0]
            for depth in depths[1:]:
                total = total + depth
            front = jnp.zeros_like(total)
            image = [jnp.zeros_like(total)] * 3
            for source in range(n_y // 2):
                before = jnp.where(rising, front, total - front - depths[source])
                seen = jnp.exp(-before)
                image = [image[c] + got[source, view, c, tile] * seen for c in range(3)]
                front = front + depths[source]
            for c in range(3):
                img_ref[view, c, :, lanes] = image[c]
            tr_ref[view, :, lanes] = jnp.exp(-total)

    for other in range(n_y // 2):
        hand(other).wait_send()

        @pl.when(other != pair)
        def _():
            share(other, pair).wait_send()
    out_copy.wait()


def deliver(*refs):
    count = (len(refs) - 1) // 2
    sem = refs[-1]
    copies = []
    for src, dst in zip(refs[:count], refs[count:-1]):
        pieces = CHUNKS if src.shape[0] % CHUNKS == 0 else 1
        size = src.shape[0] // pieces
        for piece in range(pieces):
            cut = pl.ds(piece * size, size)
            copies.append(pltpu.make_async_copy(src.at[cut], dst.at[cut], sem.at[len(copies)]))
    for copy in copies:
        copy.start()
    for copy in copies:
        copy.wait()


def per_device(n_x, n_y, scalar_field, diffusivity, reaction_rate, shear_offsets, depth_order,
               tf_centres, tf_colour, tf_opacity):
    nx, ny, nz = scalar_field.shape
    views, bumps = depth_order.shape[0], tf_centres.shape[0]
    rows, ztiles = nx // n_y, nz // LANES
    f32 = jnp.float32
    vmem = pl.BlockSpec(memory_space=pltpu.VMEM)
    far = pl.BlockSpec(memory_space=pl.ANY)
    pinned = pl.BlockSpec(memory_space=pltpu.HBM)

    def space(*shape):
        return pltpu.VMEM(shape, f32)

    x_face, y_face = space(ny, nz), space(nx, nz)
    x_faces, y_faces = space(STEPS, ny, nz), space(STEPS, nx, nz)
    shares = space(n_y, views, 4, ztiles, rows, LANES)
    halves = space(n_y // 2, views, 4, ztiles, rows, LANES)
    results = (
        jax.ShapeDtypeStruct((nx, ny, nz), f32),
        jax.ShapeDtypeStruct((views, 3, rows, nz), f32),
        jax.ShapeDtypeStruct((views, rows, nz), f32),
    )
    made = pl.pallas_call(
        functools.partial(kernel, n_x, n_y),
        out_shape=results,
        in_specs=[pinned] * 8,
        out_specs=(far, vmem, vmem),
        scratch_shapes=[
            space(2, nx, ny + SUB, nz), space(nx, ny + SUB, nz),
            x_faces, x_faces, x_face, x_face,
            y_faces, y_faces, y_faces, y_faces,
            y_face, y_face, y_face, y_face, y_face, y_face,
            space(ztiles + 1, ny * nx, LANES), space(ztiles + 1, ny * nx, LANES),
            shares, halves, halves, halves,
            space(views * ztiles, SUB, LANES), space(bumps, SUB, LANES),
            space(bumps, SUB, LANES), space(3, bumps, SUB, LANES),
            space(nx, ny, nz), space(nx, ny, nz),
            pltpu.SMEM(shear_offsets.shape, jnp.int32), pltpu.VMEM(depth_order.shape, jnp.int32),
            pltpu.SMEM(tf_centres.shape, f32), pltpu.SMEM(tf_colour.shape, f32),
            pltpu.SMEM(tf_opacity.shape, f32),
            pltpu.SemaphoreType.DMA((STEPS + 1, 4)), pltpu.SemaphoreType.DMA((STEPS + 1, 4)),
            *[pltpu.SemaphoreType.DMA((n_y // 2,))] * 4,
            pltpu.SemaphoreType.DMA, pltpu.SemaphoreType.DMA((8,)),
        ],
        compiler_params=pltpu.CompilerParams(
            collective_id=0, has_side_effects=True, vmem_limit_bytes=60 * 1024 * 1024),
    )(scalar_field, diffusivity, reaction_rate, shear_offsets, depth_order,
      tf_centres, tf_colour, tf_opacity)
    return pl.pallas_call(
        deliver,
        out_shape=results,
        in_specs=[far] * 3,
        out_specs=(far,) * 3,
        scratch_shapes=[pltpu.SemaphoreType.DMA((3 * CHUNKS,))],
        compiler_params=pltpu.CompilerParams(vmem_limit_bytes=60 * 1024 * 1024),
    )(*made)


def solution(mesh):
    grid = P("sx", "sy", None)
    return jax.shard_map(
        functools.partial(per_device, mesh.shape["sx"], mesh.shape["sy"]),
        mesh=mesh,
        in_specs=(grid, grid, grid, P(), P(), P(), P(), P()),
        out_specs=(grid, P(None, None, ("sx", "sy"), None), P(None, ("sx", "sy"), None)),
        check_vma=False,
    )
```

```python
import functools
import math

import jax
import jax.numpy as jnp
from jax import lax
from jax.experimental import pallas as pl
from jax.experimental.pallas import tpu as pltpu
from jax.sharding import PartitionSpec as P

STEPS = 4
DIFF_GAIN = 0.4
SHARPNESS = 2.0
LOG2E = math.log2(math.e)
SCALE = SHARPNESS * math.sqrt(LOG2E)
MESH = pl.DeviceIdType.MESH
LANES = 128
SUB = 8
UNROLL = 32
CHUNKS = 8
WIDE = 2


def conduct(diff, field):
    return diff * (1.0 + DIFF_GAIN * jnp.tanh(field))


def kernel(
    n_x, n_y,
    u_hbm, d_hbm, r_hbm, off_hbm, ord_hbm, cen_hbm, col_hbm, opa_hbm,
    f_ref, img_ref, tr_ref,
    field, cond, x_lo, x_hi, dx_lo, dx_hi, p_lo, p_hi, y_lo, y_hi,
    dp_lo, dp_hi, dy_lo, dy_hi, del_lo, del_hi, tall, slope,
    part, mate, both, got, sgn_ref, c2_ref, wop_ref, wcol_ref,
    d_ref, r_ref, off_ref, ord_ref, cen_ref, col_ref, opa_ref,
    halo_send, halo_recv, mate_send, mate_recv, part_send, part_recv,
    out_sem, in_sem,
):
    nx, ny, nz = u_hbm.shape
    views = ord_ref.shape[0]
    bumps = cen_ref.shape[0]
    ztiles = nz // LANES
    rows = part.shape[4]
    per_group = SUB // rows
    groups = nx // SUB
    ix, iy = lax.axis_index("sx"), lax.axis_index("sy")

    fetches = [
        pltpu.make_async_copy(src, dst, in_sem.at[i]) for i, (src, dst) in enumerate((
            (u_hbm, field.at[0, :, pl.ds(0, ny)]), (d_hbm, d_ref), (r_hbm, r_ref),
            (off_hbm, off_ref), (ord_hbm, ord_ref), (cen_hbm, cen_ref), (col_hbm, col_ref),
            (opa_hbm, opa_ref)))
    ]
    for fetch in fetches:
        fetch.start()

    barrier = pltpu.get_barrier_semaphore()
    for hop in range(1, n_y):
        pl.semaphore_signal(
            barrier, inc=1, device_id={"sy": lax.rem(iy + hop, n_y)}, device_id_type=MESH)

    @pl.when(ix > 0)
    def _():
        pl.semaphore_signal(barrier, inc=1, device_id={"sx": ix - 1}, device_id_type=MESH)

    @pl.when(ix < n_x - 1)
    def _():
        pl.semaphore_signal(barrier, inc=1, device_id={"sx": ix + 1}, device_id_type=MESH)

    sides = [
        (ix > 0, {"sx": ix - 1}, 0, 1),
        (ix < n_x - 1, {"sx": ix + 1}, 1, 0),
        (iy > 0, {"sy": iy - 1}, 2, 3),
        (iy < n_y - 1, {"sy": iy + 1}, 3, 2),
    ]
    landings = [x_lo, x_hi, y_lo, y_hi]
    diff_landings = [dx_lo, dx_hi, dy_lo, dy_hi]

    def halo(step, side):
        exists, neighbour, here, there = sides[side]
        if step == STEPS:
            src = [d_ref.at[0], d_ref.at[nx - 1], dp_lo, dp_hi][side]
            dst, own = diff_landings[there], diff_landings[here]
        else:
            now = step % 2
            src = [
                field.at[now, 0, pl.ds(0, ny)], field.at[now, nx - 1, pl.ds(0, ny)],
                p_lo.at[step], p_hi.at[step],
            ][side]
            dst, own = landings[there].at[step], landings[here].at[step]
        go = pltpu.make_async_remote_copy(
            src_ref=src, dst_ref=dst, send_sem=halo_send.at[step, here],
            recv_sem=halo_recv.at[step, there], device_id=neighbour, device_id_type=MESH)
        come = pltpu.make_async_remote_copy(
            src_ref=src, dst_ref=own, send_sem=halo_send.at[step, here],
            recv_sem=halo_recv.at[step, here], device_id=neighbour, device_id_type=MESH)
        return exists, go, come

    def start_halos(step):
        for side in range(4):
            exists, go, _ = halo(step, side)
            pl.when(exists)(go.start)

    def wait_halos(step):
        for side in range(4):
            exists, go, come = halo(step, side)

            @pl.when(exists)
            def _():
                come.wait_recv()
                go.wait_send()

    for side in range(4):
        @pl.when(jnp.logical_not(sides[side][0]))
        def _():
            landings[side][...] = jnp.zeros_like(landings[side])
            diff_landings[side][...] = jnp.zeros_like(diff_landings[side])

    fetches[0].wait()
    fetches[1].wait()

    @pl.loop(0, groups, unroll=True)
    def _(block):
        base = pl.multiple_of(block * SUB, SUB)
        for ref, row, out in (
            (field.at[0], 0, p_lo.at[0]), (field.at[0], ny - 1, p_hi.at[0]),
            (d_ref, 0, dp_lo), (d_ref, ny - 1, dp_hi),
        ):
            out[pl.ds(base, SUB), :] = jnp.concatenate(
                [ref[base + j, row:row + 1, :] for j in range(SUB)], axis=0)

    arrivals = (n_y - 1) + (ix > 0).astype(jnp.int32) + (ix < n_x - 1).astype(jnp.int32)
    pl.semaphore_wait(barrier, arrivals)
    start_halos(0)
    start_halos(STEPS)

    row_at = lax.broadcasted_iota(jnp.int32, (SUB, LANES), 0)
    lane = lax.broadcasted_iota(jnp.int32, (SUB, LANES), 1)
    first_row, last_row, first_lane = row_at == 0, row_at == SUB - 1, lane == 0

    for step in range(STEPS):
        now, later = step % 2, (step + 1) % 2

        @pl.loop(0, nx, unroll=8)
        def _(x):
            for t in range(ny // SUB):
                cut = pl.ds(t * SUB, SUB)
                cond[x, cut, :] = conduct(d_ref[x, cut, :], field[now, x, cut, :])

        if step == 0:
            fetches[2].wait()

        @pl.loop(0, nx, unroll=4)
        def _(x):
            below, above = jnp.maximum(x - 1, 0), jnp.minimum(x + 1, nx - 1)
            tiles = ny // SUB
            before = [None] * tiles
            for tile in range(ztiles):
                lanes = slice(tile * LANES, (tile + 1) * LANES)
                rear = slice((tile + 1) * LANES, (tile + 2) * LANES)
                up_u, up_k, carried = None, None, None
                for t in range(tiles):
                    cut = pl.ds(t * SUB, SUB)
                    u, k = field[now, x, cut, lanes], cond[x, cut, lanes]
                    change = (k + cond[below, cut, lanes]) * (field[now, below, cut, lanes] - u)
                    change += (k + cond[above, cut, lanes]) * (field[now, above, cut, lanes] - u)

                    if t == 0:
                        up_u, up_k = pltpu.roll(u, SUB - 1, 0), pltpu.roll(k, SUB - 1, 0)
                    if t < tiles - 1:
                        cut_on = pl.ds((t + 1) * SUB, SUB)
                        on_u = pltpu.roll(field[now, x, cut_on, lanes], SUB - 1, 0)
                        on_k = pltpu.roll(cond[x, cut_on, lanes], SUB - 1, 0)
                        flux = (k + jnp.where(last_row, on_k, up_k)) * (
                            jnp.where(last_row, on_u, up_u) - u)
                        up_u, up_k = on_u, on_k
                    else:
                        flux = jnp.where(last_row, 0.0, (k + up_k) * (up_u - u))
                    turned = pltpu.roll(flux, 1, 0)
                    change += flux - jnp.where(first_row, 0.0 if t == 0 else carried, turned)
                    carried = turned

                    if tile < ztiles - 1:
                        on_u, on_k = field[now, x, cut, rear], cond[x, cut, rear]
                        next_u = pltpu.roll(jnp.where(first_lane, on_u, u), LANES - 1, 1)
                        next_k = pltpu.roll(jnp.where(first_lane, on_k, k), LANES - 1, 1)
                    else:
                        next_u = pltpu.roll(jnp.where(first_lane, 0.0, u), LANES - 1, 1)
                        next_k = pltpu.roll(jnp.where(first_lane, 0.0, k), LANES - 1, 1)
                    flux = (k + next_k) * (next_u - u)
                    turned = pltpu.roll(flux, 1, 1)
                    start = k * u if tile == 0 else before[t]
                    change += flux - jnp.where(first_lane, start, turned)
                    before[t] = turned
                    field[later, x, cut, lanes] = (
                        u + 0.5 * change + r_ref[x, cut, lanes] * jnp.tanh(u))

        if step == 0:
            wait_halos(STEPS)
        wait_halos(step)
        inner = pl.ds(0, ny)
        for x, land, diff in ((0, x_lo, dx_lo), (nx - 1, x_hi, dx_hi)):
            beside = land[step]
            field[later, x, inner, :] += (
                0.5 * (cond[x, inner, :] + conduct(diff[...], beside))
                * (beside - field[now, x, inner, :]))
        for packed, own, land, diff, out in (
            (p_lo, dp_lo, y_lo, dy_lo, del_lo), (p_hi, dp_hi, y_hi, dy_hi, del_hi),
        ):
            u, beside = packed[step], land[step]
            out[...] = 0.5 * (conduct(own[...], u) + conduct(diff[...], beside)) * (beside - u)

        @pl.loop(0, groups, unroll=True)
        def _(block):
            base = pl.multiple_of(block * SUB, SUB)
            for packed, delta, row in ((p_lo, del_lo, 0), (p_hi, del_hi, ny - 1)):
                extra = delta[pl.ds(base, SUB), :]
                edge = []
                for j in range(SUB):
                    value = field[later, base + j, row:row + 1, :] + extra[j:j + 1, :]
                    field[later, base + j, row:row + 1, :] = value
                    edge.append(value)
                if step < STEPS - 1:
                    packed[step + 1, pl.ds(base, SUB), :] = jnp.concatenate(edge, axis=0)

        if step < STEPS - 1:
            start_halos(step + 1)

    last = STEPS % 2
    out_copy = pltpu.make_async_copy(field.at[last, :, pl.ds(0, ny)], f_ref, out_sem)
    out_copy.start()

    for ref in (tall, slope):
        ref[ztiles] = jnp.zeros_like(ref[ztiles])

    @pl.loop(0, nx, unroll=2)
    def _(x):
        for t in range(ny // SUB):
            value = field[last, x, pl.ds(t * SUB, SUB), :] * SCALE
            for tile in range(ztiles):
                spot = pl.ds(t * SUB * nx + x, SUB, stride=nx)
                tall[tile, spot, :] = value[:, tile * LANES:(tile + 1) * LANES]

    @pl.loop(0, ny * nx // SUB, unroll=4)
    def _(block):
        spot = pl.ds(pl.multiple_of(block * SUB, SUB), SUB)
        values = [tall[tile, spot, :] for tile in range(ztiles)]
        ahead = [pltpu.roll(value, LANES - 1, 1) for value in values] + [0.0]
        for tile in range(ztiles):
            beside = jnp.where(lane == LANES - 1, ahead[tile + 1], ahead[tile])
            slope[tile, spot, :] = beside - values[tile]

    for fetch in fetches[3:]:
        fetch.wait()
    for view in range(views):
        for tile in range(ztiles):
            order = ord_ref[view:view + 1, tile * LANES:(tile + 1) * LANES]
            sign = jnp.where(order == 0, -1.0, 1.0)
            sgn_ref[view * ztiles + tile] = jnp.broadcast_to(sign, (SUB, LANES))
    for bump in range(bumps):
        centre = jnp.full((SUB, LANES), cen_ref[bump] * SCALE, jnp.float32)
        factor = jnp.exp2(-centre * centre)
        c2_ref[bump] = 2.0 * centre
        wop_ref[bump] = opa_ref[bump] * factor
        for channel in range(3):
            wcol_ref[channel, bump] = col_ref[channel, bump] * factor

    pairs = ztiles // WIDE

    def render(group, view, first):
        rate = [sgn_ref[view * ztiles + first + a] * LOG2E for a in range(WIDE)]
        c2 = [c2_ref[b] for b in range(bumps)]

        def plane(y, carry):
            offset = off_ref[view, iy * ny + y]
            whole = offset >> 2
            frac = (offset & 3).astype(jnp.float32) * 0.25
            spot = pl.ds(pl.multiple_of(y * nx + group * SUB, SUB), SUB)
            turned = []
            for a in range(WIDE + 1):
                mixed = tall[first + a, spot, :] + frac * slope[first + a, spot, :]
                turned.append(pltpu.roll(mixed, (LANES - whole) & (LANES - 1), 1))
            inside = lane < LANES - whole
            result = []
            wop = [wop_ref[b] for b in range(bumps)]
            for a in range(WIDE):
                sums, depth, light = carry[a]
                s = jnp.where(inside, turned[a], turned[a + 1])
                bump = [jnp.exp2(s * (c2[b] - s)) for b in range(bumps)]
                terms = [wop[b] * bump[b] for b in range(bumps)]
                while len(terms) > 1:
                    terms = [i + j for i, j in zip(terms[::2], terms[1::2])]
                depth = depth + terms[0]
                new = jnp.exp2(rate[a] * depth)
                step = new - light
                sums = tuple(sums[b] + step * bump[b] for b in range(bumps))
                result.append((sums, depth, new))
            return tuple(result)

        unroll = min(UNROLL, ny)

        def several(i, carry):
            for j in range(unroll):
                carry = plane(i * unroll + j, carry)
            return carry

        zero = jnp.zeros((SUB, LANES), jnp.float32)
        start = tuple(((zero,) * bumps, zero, zero + 1.0) for a in range(WIDE))
        ended = lax.fori_loop(0, ny // unroll, several, start)
        for a in range(WIDE):
            sums, depth, light = ended[a]
            sign = sgn_ref[view * ztiles + first + a]
            factor = jnp.where(sign > 0.0, jnp.exp(-depth), -1.0)
            values = []
            for channel in range(3):
                total = wcol_ref[channel, 0] * sums[0]
                for b in range(1, bumps):
                    total += wcol_ref[channel, b] * sums[b]
                values.append(total * factor)
            values.append(depth)
            for j in range(per_group):
                for channel, value in enumerate(values):
                    part[group * per_group + j, view, channel, first + a] = (
                        value[j * rows:(j + 1) * rows])

    core, pair = lax.rem(iy, 2), iy // 2
    twin = iy + 1 - 2 * core
    group_pairs = per_group // 2
    flip = (1 - 2 * core).astype(jnp.float32)

    def hand(which):
        return pltpu.make_async_remote_copy(
            src_ref=part.at[2 * which + 1 - core], dst_ref=mate.at[which],
            send_sem=mate_send.at[which], recv_sem=mate_recv.at[which],
            device_id={"sy": twin}, device_id_type=MESH)

    def share(which, slot):
        return pltpu.make_async_remote_copy(
            src_ref=both.at[which], dst_ref=got.at[slot], send_sem=part_send.at[which],
            recv_sem=part_recv.at[slot], device_id={"sy": 2 * which + core}, device_id_type=MESH)

    def merge(which):
        hand(which).wait_recv()
        for view in range(views):
            for tile in range(ztiles):
                mine_first = sgn_ref[view * ztiles + tile][:rows] * flip < 0.0
                mine = [part[2 * which + core, view, c, tile] for c in range(4)]
                other = [mate[which, view, c, tile] for c in range(4)]
                dim = jnp.exp(-jnp.where(mine_first, mine[3], other[3]))
                for c in range(3):
                    near = jnp.where(mine_first, mine[c], other[c])
                    far = jnp.where(mine_first, other[c], mine[c])
                    both[which, view, c, tile] = near + dim * far
                both[which, view, 3, tile] = mine[3] + other[3]

    def finish(group):
        for j in range(group_pairs):
            which = group * group_pairs + j
            merge(which)

            @pl.when(which != pair)
            def _():
                share(which, pair).start()

            @pl.when(which == pair)
            def _():
                got[pair] = both[pair]

    own_group = iy // per_group
    early = min(2, views * pairs)

    @pl.loop(0, groups)
    def _(turn):
        group = lax.rem(own_group + 1 + turn, groups)

        def item_at(item):
            render(group, item // pairs, lax.rem(item, pairs) * WIDE)

        pl.loop(0, early)(item_at)

        @pl.when(turn > 0)
        def _():
            finish(lax.rem(own_group + turn, groups))

        pl.loop(early, views * pairs)(item_at)
        for j in range(group_pairs):
            hand(group * group_pairs + j).start()

    finish(own_group)
    for other in range(n_y // 2):
        @pl.when(other != pair)
        def _():
            share(other, other).wait_recv()

    for view in range(views):
        for tile in range(ztiles):
            lanes = slice(tile * LANES, (tile + 1) * LANES)
            rising = sgn_ref[view * ztiles + tile][:rows] < 0.0
            depths = [got[source, view, 3, tile] for source in range(n_y // 2)]
            total = depths[0]
            for depth in depths[1:]:
                total = total + depth
            front = jnp.zeros_like(total)
            image = [jnp.zeros_like(total)] * 3
            for source in range(n_y // 2):
                before = jnp.where(rising, front, total - front - depths[source])
                seen = jnp.exp(-before)
                image = [image[c] + got[source, view, c, tile] * seen for c in range(3)]
                front = front + depths[source]
            for c in range(3):
                img_ref[view, c, :, lanes] = image[c]
            tr_ref[view, :, lanes] = jnp.exp(-total)

    for other in range(n_y // 2):
        hand(other).wait_send()

        @pl.when(other != pair)
        def _():
            share(other, pair).wait_send()
    out_copy.wait()


def deliver(*refs):
    count = (len(refs) - 2) // 3
    sem_in, sem_out = refs[-2:]
    copies = []
    for src, dst, held in zip(refs[:count], refs[count:2 * count], refs[2 * count:-2]):
        pieces = CHUNKS if src.shape[0] % CHUNKS == 0 else 1
        size = src.shape[0] // pieces
        for piece in range(pieces):
            cut, at = pl.ds(piece * size, size), len(copies)
            copies.append((
                pltpu.make_async_copy(src.at[cut], held.at[cut], sem_in.at[at]),
                pltpu.make_async_copy(held.at[cut], dst.at[cut], sem_out.at[at])))
    for come, _ in copies:
        come.start()
    for come, go in copies:
        come.wait()
        go.start()
    for _, go in copies:
        go.wait()


def per_device(n_x, n_y, scalar_field, diffusivity, reaction_rate, shear_offsets, depth_order,
               tf_centres, tf_colour, tf_opacity):
    nx, ny, nz = scalar_field.shape
    views, bumps = depth_order.shape[0], tf_centres.shape[0]
    rows, ztiles = nx // n_y, nz // LANES
    f32 = jnp.float32
    vmem = pl.BlockSpec(memory_space=pltpu.VMEM)
    far = pl.BlockSpec(memory_space=pl.ANY)
    pinned = pl.BlockSpec(memory_space=pltpu.HBM)

    def space(*shape):
        return pltpu.VMEM(shape, f32)

    x_face, y_face = space(ny, nz), space(nx, nz)
    x_faces, y_faces = space(STEPS, ny, nz), space(STEPS, nx, nz)
    shares = space(n_y, views, 4, ztiles, rows, LANES)
    halves = space(n_y // 2, views, 4, ztiles, rows, LANES)
    results = (
        jax.ShapeDtypeStruct((nx, ny, nz), f32),
        jax.ShapeDtypeStruct((views, 3, rows, nz), f32),
        jax.ShapeDtypeStruct((views, rows, nz), f32),
    )
    made = pl.pallas_call(
        functools.partial(kernel, n_x, n_y),
        out_shape=results,
        in_specs=[pinned] * 8,
        out_specs=(far, vmem, vmem),
        scratch_shapes=[
            space(2, nx, ny + SUB, nz), space(nx, ny + SUB, nz),
            x_faces, x_faces, x_face, x_face,
            y_faces, y_faces, y_faces, y_faces,
            y_face, y_face, y_face, y_face, y_face, y_face,
            space(ztiles + 1, ny * nx, LANES), space(ztiles + 1, ny * nx, LANES),
            shares, halves, halves, halves,
            space(views * ztiles, SUB, LANES), space(bumps, SUB, LANES),
            space(bumps, SUB, LANES), space(3, bumps, SUB, LANES),
            space(nx, ny, nz), space(nx, ny, nz),
            pltpu.SMEM(shear_offsets.shape, jnp.int32), pltpu.VMEM(depth_order.shape, jnp.int32),
            pltpu.SMEM(tf_centres.shape, f32), pltpu.SMEM(tf_colour.shape, f32),
            pltpu.SMEM(tf_opacity.shape, f32),
            pltpu.SemaphoreType.DMA((STEPS + 1, 4)), pltpu.SemaphoreType.DMA((STEPS + 1, 4)),
            *[pltpu.SemaphoreType.DMA((n_y // 2,))] * 4,
            pltpu.SemaphoreType.DMA, pltpu.SemaphoreType.DMA((8,)),
        ],
        compiler_params=pltpu.CompilerParams(
            collective_id=0, has_side_effects=True, vmem_limit_bytes=60 * 1024 * 1024),
    )(scalar_field, diffusivity, reaction_rate, shear_offsets, depth_order,
      tf_centres, tf_colour, tf_opacity)
    return pl.pallas_call(
        deliver,
        out_shape=results,
        in_specs=[far] * 3,
        out_specs=(far,) * 3,
        scratch_shapes=[space(*result.shape) for result in results]
        + [pltpu.SemaphoreType.DMA((3 * CHUNKS,))] * 2,
        compiler_params=pltpu.CompilerParams(vmem_limit_bytes=60 * 1024 * 1024),
    )(*made)


def solution(mesh):
    grid = P("sx", "sy", None)
    return jax.shard_map(
        functools.partial(per_device, mesh.shape["sx"], mesh.shape["sy"]),
        mesh=mesh,
        in_specs=(grid, grid, grid, P(), P(), P(), P(), P()),
        out_specs=(grid, P(None, None, ("sx", "sy"), None), P(None, ("sx", "sy"), None)),
        check_vma=False,
    )
```

```python
import functools
import math

import jax
import jax.numpy as jnp
from jax import lax
from jax.experimental import pallas as pl
from jax.experimental.pallas import tpu as pltpu
from jax.sharding import PartitionSpec as P

STEPS = 4
DIFF_GAIN = 0.4
SHARPNESS = 2.0
LOG2E = math.log2(math.e)
SCALE = SHARPNESS * math.sqrt(LOG2E)
MESH = pl.DeviceIdType.MESH
LANES = 128
SUB = 8
UNROLL = 32
CHUNKS = 8
WIDE = 2


def conduct(diff, field):
    return diff * (1.0 + DIFF_GAIN * jnp.tanh(field))


def kernel(
    n_x, n_y,
    u_hbm, d_hbm, r_hbm, off_hbm, ord_hbm, cen_hbm, col_hbm, opa_hbm,
    f_ref, img_ref, tr_ref,
    field_a, field_b, cond, x_lo, x_hi, dx_lo, dx_hi, p_lo, p_hi, y_lo, y_hi,
    dp_lo, dp_hi, dy_lo, dy_hi, del_lo, del_hi, tall, slope,
    part, mate, both, got, sgn_ref, c2_ref, wop_ref, wcol_ref,
    d_ref, r_ref, off_ref, ord_ref, cen_ref, col_ref, opa_ref,
    halo_send, halo_recv, mate_send, mate_recv, part_send, part_recv,
    out_sem, in_sem,
):
    nx, ny, nz = u_hbm.shape
    fields = (field_a, field_b)
    views = ord_ref.shape[0]
    bumps = cen_ref.shape[0]
    ztiles = nz // LANES
    rows = part.shape[4]
    per_group = SUB // rows
    groups = nx // SUB
    ix, iy = lax.axis_index("sx"), lax.axis_index("sy")

    fetches = [
        pltpu.make_async_copy(src, dst, in_sem.at[i]) for i, (src, dst) in enumerate((
            (u_hbm, fields[0].at[:, pl.ds(0, ny)]), (d_hbm, d_ref), (r_hbm, r_ref),
            (off_hbm, off_ref), (ord_hbm, ord_ref), (cen_hbm, cen_ref), (col_hbm, col_ref),
            (opa_hbm, opa_ref)))
    ]
    for fetch in fetches:
        fetch.start()

    barrier = pltpu.get_barrier_semaphore()
    for hop in range(1, n_y):
        pl.semaphore_signal(
            barrier, inc=1, device_id={"sy": lax.rem(iy + hop, n_y)}, device_id_type=MESH)

    @pl.when(ix > 0)
    def _():
        pl.semaphore_signal(barrier, inc=1, device_id={"sx": ix - 1}, device_id_type=MESH)

    @pl.when(ix < n_x - 1)
    def _():
        pl.semaphore_signal(barrier, inc=1, device_id={"sx": ix + 1}, device_id_type=MESH)

    sides = [
        (ix > 0, {"sx": ix - 1}, 0, 1),
        (ix < n_x - 1, {"sx": ix + 1}, 1, 0),
        (iy > 0, {"sy": iy - 1}, 2, 3),
        (iy < n_y - 1, {"sy": iy + 1}, 3, 2),
    ]
    landings = [x_lo, x_hi, y_lo, y_hi]
    diff_landings = [dx_lo, dx_hi, dy_lo, dy_hi]

    def halo(step, side):
        exists, neighbour, here, there = sides[side]
        if step == STEPS:
            src = [d_ref.at[0], d_ref.at[nx - 1], dp_lo, dp_hi][side]
            dst, own = diff_landings[there], diff_landings[here]
        else:
            now = step % 2
            src = [
                fields[now].at[0, pl.ds(0, ny)], fields[now].at[nx - 1, pl.ds(0, ny)],
                p_lo.at[step], p_hi.at[step],
            ][side]
            dst, own = landings[there].at[step], landings[here].at[step]
        go = pltpu.make_async_remote_copy(
            src_ref=src, dst_ref=dst, send_sem=halo_send.at[step, here],
            recv_sem=halo_recv.at[step, there], device_id=neighbour, device_id_type=MESH)
        come = pltpu.make_async_remote_copy(
            src_ref=src, dst_ref=own, send_sem=halo_send.at[step, here],
            recv_sem=halo_recv.at[step, here], device_id=neighbour, device_id_type=MESH)
        return exists, go, come

    def start_halos(step):
        for side in range(4):
            exists, go, _ = halo(step, side)
            pl.when(exists)(go.start)

    def wait_halos(step):
        for side in range(4):
            exists, go, come = halo(step, side)

            @pl.when(exists)
            def _():
                come.wait_recv()
                go.wait_send()

    for side in range(4):
        @pl.when(jnp.logical_not(sides[side][0]))
        def _():
            landings[side][...] = jnp.zeros_like(landings[side])
            diff_landings[side][...] = jnp.zeros_like(diff_landings[side])

    fetches[0].wait()
    fetches[1].wait()

    @pl.loop(0, groups, unroll=True)
    def _(block):
        base = pl.multiple_of(block * SUB, SUB)
        for ref, row, out in (
            (fields[0], 0, p_lo.at[0]), (fields[0], ny - 1, p_hi.at[0]),
            (d_ref, 0, dp_lo), (d_ref, ny - 1, dp_hi),
        ):
            out[pl.ds(base, SUB), :] = jnp.concatenate(
                [ref[base + j, row:row + 1, :] for j in range(SUB)], axis=0)

    arrivals = (n_y - 1) + (ix > 0).astype(jnp.int32) + (ix < n_x - 1).astype(jnp.int32)
    pl.semaphore_wait(barrier, arrivals)
    start_halos(0)
    start_halos(STEPS)

    row_at = lax.broadcasted_iota(jnp.int32, (SUB, nz), 0)
    col_at = lax.broadcasted_iota(jnp.int32, (SUB, nz), 1)

    for step in range(STEPS):
        now, later = step % 2, (step + 1) % 2

        @pl.loop(0, nx, unroll=8)
        def _(x):
            for t in range(ny // SUB):
                cut = pl.ds(t * SUB, SUB)
                cond[x, cut, :] = conduct(d_ref[x, cut, :], fields[now][x, cut, :])

        if step == 0:
            fetches[2].wait()

        @pl.loop(0, nx, unroll=4)
        def _(x):
            below, above = jnp.maximum(x - 1, 0), jnp.minimum(x + 1, nx - 1)
            tiles = ny // SUB
            cuts = [pl.ds(t * SUB, SUB) for t in range(tiles)]
            us = [fields[now][x, cut, :] for cut in cuts]
            ks = [cond[x, cut, :] for cut in cuts]
            up_u = [pltpu.roll(u, SUB - 1, 0) for u in us]
            up_k = [pltpu.roll(k, SUB - 1, 0) for k in ks]
            carried, made = None, []
            for t, cut in enumerate(cuts):
                u, k = us[t], ks[t]
                change = (k + cond[below, cut, :]) * (fields[now][below, cut, :] - u)
                change += (k + cond[above, cut, :]) * (fields[now][above, cut, :] - u)
                if t < tiles - 1:
                    next_u = jnp.where(row_at == SUB - 1, up_u[t + 1], up_u[t])
                    next_k = jnp.where(row_at == SUB - 1, up_k[t + 1], up_k[t])
                else:
                    next_u, next_k = up_u[t], up_k[t]
                flux = (k + next_k) * (next_u - u)
                if t == tiles - 1:
                    flux = jnp.where(row_at == SUB - 1, 0.0, flux)
                turned = pltpu.roll(flux, 1, 0)
                change += flux - jnp.where(row_at == 0, 0.0 if t == 0 else carried, turned)
                carried = turned
                ku = k * u
                right_u, right_k = pltpu.roll(u, nz - 1, 1), pltpu.roll(k, nz - 1, 1)
                flux = jnp.where(col_at == nz - 1, -ku, (k + right_k) * (right_u - u))
                change += flux - jnp.where(col_at == 0, ku, pltpu.roll(flux, 1, 1))
                made.append(u + 0.5 * change + r_ref[x, cut, :] * jnp.tanh(u))
            for cut, value in zip(cuts, made):
                fields[later][x, cut, :] = value

        if step == 0:
            wait_halos(STEPS)
        wait_halos(step)
        inner = pl.ds(0, ny)
        for x, land, diff in ((0, x_lo, dx_lo), (nx - 1, x_hi, dx_hi)):
            beside = land[step]
            fields[later][x, inner, :] += (
                0.5 * (cond[x, inner, :] + conduct(diff[...], beside))
                * (beside - fields[now][x, inner, :]))
        for packed, own, land, diff, out in (
            (p_lo, dp_lo, y_lo, dy_lo, del_lo), (p_hi, dp_hi, y_hi, dy_hi, del_hi),
        ):
            u, beside = packed[step], land[step]
            out[...] = 0.5 * (conduct(own[...], u) + conduct(diff[...], beside)) * (beside - u)

        @pl.loop(0, groups, unroll=True)
        def _(block):
            base = pl.multiple_of(block * SUB, SUB)
            for packed, delta, row in ((p_lo, del_lo, 0), (p_hi, del_hi, ny - 1)):
                extra = delta[pl.ds(base, SUB), :]
                edge = [
                    fields[later][base + j, row:row + 1, :] + extra[j:j + 1, :]
                    for j in range(SUB)]
                for j in range(SUB):
                    fields[later][base + j, row:row + 1, :] = edge[j]
                if step < STEPS - 1:
                    packed[step + 1, pl.ds(base, SUB), :] = jnp.concatenate(edge, axis=0)

        if step < STEPS - 1:
            start_halos(step + 1)

    last = STEPS % 2
    out_copy = pltpu.make_async_copy(fields[last].at[:, pl.ds(0, ny)], f_ref, out_sem)
    out_copy.start()

    for ref in (tall, slope):
        ref[ztiles] = jnp.zeros_like(ref[ztiles])

    @pl.loop(0, nx, unroll=2)
    def _(x):
        for t in range(ny // SUB):
            value = fields[last][x, pl.ds(t * SUB, SUB), :] * SCALE
            for tile in range(ztiles):
                spot = pl.ds(t * SUB * nx + x, SUB, stride=nx)
                tall[tile, spot, :] = value[:, tile * LANES:(tile + 1) * LANES]

    lane = lax.broadcasted_iota(jnp.int32, (SUB, LANES), 1)

    @pl.loop(0, ny * nx // SUB, unroll=4)
    def _(block):
        spot = pl.ds(pl.multiple_of(block * SUB, SUB), SUB)
        values = [tall[tile, spot, :] for tile in range(ztiles)]
        ahead = [pltpu.roll(value, LANES - 1, 1) for value in values] + [0.0]
        for tile in range(ztiles):
            beside = jnp.where(lane == LANES - 1, ahead[tile + 1], ahead[tile])
            slope[tile, spot, :] = beside - values[tile]

    for fetch in fetches[3:]:
        fetch.wait()
    for view in range(views):
        for tile in range(ztiles):
            order = ord_ref[view:view + 1, tile * LANES:(tile + 1) * LANES]
            sign = jnp.where(order == 0, -1.0, 1.0)
            sgn_ref[view * ztiles + tile] = jnp.broadcast_to(sign, (SUB, LANES))
    for bump in range(bumps):
        centre = jnp.full((SUB, LANES), cen_ref[bump] * SCALE, jnp.float32)
        factor = jnp.exp2(-centre * centre)
        c2_ref[bump] = 2.0 * centre
        wop_ref[bump] = opa_ref[bump] * factor
        for channel in range(3):
            wcol_ref[channel, bump] = col_ref[channel, bump] * factor

    pairs = ztiles // WIDE

    def render(group, view, first):
        rate = [sgn_ref[view * ztiles + first + a] * LOG2E for a in range(WIDE)]

        def plane(y, carry):
            offset = off_ref[view, iy * ny + y]
            whole = offset >> 2
            frac = (offset & 3).astype(jnp.float32) * 0.25
            spot = pl.ds(pl.multiple_of(y * nx + group * SUB, SUB), SUB)
            turned = []
            for a in range(WIDE + 1):
                mixed = tall[first + a, spot, :] + frac * slope[first + a, spot, :]
                turned.append(pltpu.roll(mixed, (LANES - whole) & (LANES - 1), 1))
            inside = lane < LANES - whole
            result = []
            for a in range(WIDE):
                sums, depth, light = carry[a]
                s = jnp.where(inside, turned[a], turned[a + 1])
                bump = [jnp.exp2(s * (c2_ref[b] - s)) for b in range(bumps)]
                terms = [wop_ref[b] * bump[b] for b in range(bumps)]
                while len(terms) > 1:
                    terms = [i + j for i, j in zip(terms[::2], terms[1::2])]
                depth = depth + terms[0]
                new = jnp.exp2(rate[a] * depth)
                step = new - light
                sums = tuple(sums[b] + step * bump[b] for b in range(bumps))
                result.append((sums, depth, new))
            return tuple(result)

        unroll = min(UNROLL, ny)

        def several(i, carry):
            for j in range(unroll):
                carry = plane(i * unroll + j, carry)
            return carry

        zero = jnp.zeros((SUB, LANES), jnp.float32)
        start = tuple(((zero,) * bumps, zero, zero + 1.0) for a in range(WIDE))
        ended = lax.fori_loop(0, ny // unroll, several, start)
        for a in range(WIDE):
            sums, depth, light = ended[a]
            sign = sgn_ref[view * ztiles + first + a]
            factor = jnp.where(sign > 0.0, jnp.exp(-depth), -1.0)
            values = []
            for channel in range(3):
                total = wcol_ref[channel, 0] * sums[0]
                for b in range(1, bumps):
                    total += wcol_ref[channel, b] * sums[b]
                values.append(total * factor)
            values.append(depth)
            for j in range(per_group):
                for channel, value in enumerate(values):
                    part[group * per_group + j, view, channel, first + a] = (
                        value[j * rows:(j + 1) * rows])

    core, pair = lax.rem(iy, 2), iy // 2
    twin = iy + 1 - 2 * core
    group_pairs = per_group // 2
    flip = (1 - 2 * core).astype(jnp.float32)

    def hand(which):
        return pltpu.make_async_remote_copy(
            src_ref=part.at[2 * which + 1 - core], dst_ref=mate.at[which],
            send_sem=mate_send.at[which], recv_sem=mate_recv.at[which],
            device_id={"sy": twin}, device_id_type=MESH)

    def share(which, slot):
        return pltpu.make_async_remote_copy(
            src_ref=both.at[which], dst_ref=got.at[slot], send_sem=part_send.at[which],
            recv_sem=part_recv.at[slot], device_id={"sy": 2 * which + core}, device_id_type=MESH)

    def merge(which):
        hand(which).wait_recv()
        for view in range(views):
            for tile in range(ztiles):
                mine_first = sgn_ref[view * ztiles + tile][:rows] * flip < 0.0
                mine = [part[2 * which + core, view, c, tile] for c in range(4)]
                other = [mate[which, view, c, tile] for c in range(4)]
                dim = jnp.exp(-jnp.where(mine_first, mine[3], other[3]))
                for c in range(3):
                    near = jnp.where(mine_first, mine[c], other[c])
                    far = jnp.where(mine_first, other[c], mine[c])
                    both[which, view, c, tile] = near + dim * far
                both[which, view, 3, tile] = mine[3] + other[3]

    def finish(group):
        for j in range(group_pairs):
            which = group * group_pairs + j
            merge(which)

            @pl.when(which != pair)
            def _():
                share(which, pair).start()

            @pl.when(which == pair)
            def _():
                got[pair] = both[pair]

    own_group = iy // per_group
    early = min(2, views * pairs)

    @pl.loop(0, groups)
    def _(turn):
        group = lax.rem(own_group + 1 + turn, groups)

        def item_at(item):
            render(group, item // pairs, lax.rem(item, pairs) * WIDE)

        pl.loop(0, early)(item_at)

        @pl.when(turn > 0)
        def _():
            finish(lax.rem(own_group + turn, groups))

        pl.loop(early, views * pairs)(item_at)
        for j in range(group_pairs):
            hand(group * group_pairs + j).start()

    finish(own_group)
    for other in range(n_y // 2):
        @pl.when(other != pair)
        def _():
            share(other, other).wait_recv()

    for view in range(views):
        for tile in range(ztiles):
            lanes = slice(tile * LANES, (tile + 1) * LANES)
            rising = sgn_ref[view * ztiles + tile][:rows] < 0.0
            depths = [got[source, view, 3, tile] for source in range(n_y // 2)]
            total = depths[0]
            for depth in depths[1:]:
                total = total + depth
            front = jnp.zeros_like(total)
            image = [jnp.zeros_like(total)] * 3
            for source in range(n_y // 2):
                before = jnp.where(rising, front, total - front - depths[source])
                seen = jnp.exp(-before)
                image = [image[c] + got[source, view, c, tile] * seen for c in range(3)]
                front = front + depths[source]
            for c in range(3):
                img_ref[view, c, :, lanes] = image[c]
            tr_ref[view, :, lanes] = jnp.exp(-total)

    for other in range(n_y // 2):
        hand(other).wait_send()

        @pl.when(other != pair)
        def _():
            share(other, pair).wait_send()
    out_copy.wait()


def deliver(*refs):
    count = (len(refs) - 2) // 3
    sem_in, sem_out = refs[-2:]
    copies = []
    for src, dst, held in zip(refs[:count], refs[count:2 * count], refs[2 * count:-2]):
        pieces = CHUNKS if src.shape[0] % CHUNKS == 0 else 1
        size = src.shape[0] // pieces
        for piece in range(pieces):
            cut, at = pl.ds(piece * size, size), len(copies)
            copies.append((
                pltpu.make_async_copy(src.at[cut], held.at[cut], sem_in.at[at]),
                pltpu.make_async_copy(held.at[cut], dst.at[cut], sem_out.at[at])))
    for come, _ in copies:
        come.start()
    for come, go in copies:
        come.wait()
        go.start()
    for _, go in copies:
        go.wait()


def per_device(n_x, n_y, scalar_field, diffusivity, reaction_rate, shear_offsets, depth_order,
               tf_centres, tf_colour, tf_opacity):
    nx, ny, nz = scalar_field.shape
    views, bumps = depth_order.shape[0], tf_centres.shape[0]
    rows, ztiles = nx // n_y, nz // LANES
    f32 = jnp.float32
    vmem = pl.BlockSpec(memory_space=pltpu.VMEM)
    far = pl.BlockSpec(memory_space=pl.ANY)
    pinned = pl.BlockSpec(memory_space=pltpu.HBM)

    def space(*shape):
        return pltpu.VMEM(shape, f32)

    x_face, y_face = space(ny, nz), space(nx, nz)
    x_faces, y_faces = space(STEPS, ny, nz), space(STEPS, nx, nz)
    shares = space(n_y, views, 4, ztiles, rows, LANES)
    halves = space(n_y // 2, views, 4, ztiles, rows, LANES)
    results = (
        jax.ShapeDtypeStruct((nx, ny, nz), f32),
        jax.ShapeDtypeStruct((views, 3, rows, nz), f32),
        jax.ShapeDtypeStruct((views, rows, nz), f32),
    )
    made = pl.pallas_call(
        functools.partial(kernel, n_x, n_y),
        out_shape=results,
        in_specs=[pinned] * 8,
        out_specs=(far, vmem, vmem),
        scratch_shapes=[
            space(nx, ny, nz), space(nx, ny, nz), space(nx, ny, nz),
            x_faces, x_faces, x_face, x_face,
            y_faces, y_faces, y_faces, y_faces,
            y_face, y_face, y_face, y_face, y_face, y_face,
            space(ztiles + 1, ny * nx, LANES), space(ztiles + 1, ny * nx, LANES),
            shares, halves, halves, halves,
            space(views * ztiles, SUB, LANES), space(bumps, SUB, LANES),
            space(bumps, SUB, LANES), space(3, bumps, SUB, LANES),
            space(nx, ny, nz), space(nx, ny, nz),
            pltpu.SMEM(shear_offsets.shape, jnp.int32), pltpu.VMEM(depth_order.shape, jnp.int32),
            pltpu.SMEM(tf_centres.shape, f32), pltpu.SMEM(tf_colour.shape, f32),
            pltpu.SMEM(tf_opacity.shape, f32),
            pltpu.SemaphoreType.DMA((STEPS + 1, 4)), pltpu.SemaphoreType.DMA((STEPS + 1, 4)),
            *[pltpu.SemaphoreType.DMA((n_y // 2,))] * 4,
            pltpu.SemaphoreType.DMA, pltpu.SemaphoreType.DMA((8,)),
        ],
        compiler_params=pltpu.CompilerParams(
            collective_id=0, has_side_effects=True, vmem_limit_bytes=60 * 1024 * 1024),
    )(scalar_field, diffusivity, reaction_rate, shear_offsets, depth_order,
      tf_centres, tf_colour, tf_opacity)
    return pl.pallas_call(
        deliver,
        out_shape=results,
        in_specs=[far] * 3,
        out_specs=(far,) * 3,
        scratch_shapes=[space(*result.shape) for result in results]
        + [pltpu.SemaphoreType.DMA((3 * CHUNKS,))] * 2,
        compiler_params=pltpu.CompilerParams(vmem_limit_bytes=60 * 1024 * 1024),
    )(*made)


def solution(mesh):
    grid = P("sx", "sy", None)
    return jax.shard_map(
        functools.partial(per_device, mesh.shape["sx"], mesh.shape["sy"]),
        mesh=mesh,
        in_specs=(grid, grid, grid, P(), P(), P(), P(), P()),
        out_specs=(grid, P(None, None, ("sx", "sy"), None), P(None, ("sx", "sy"), None)),
        check_vma=False,
    )
```
